32 devices in a mesh: blk: 16 (over z, x, core), rep: 2 (over y).
Axes of the slice: x: 2, y: 2, z: 4, core: 2. Of those that a mesh axis runs over, the one named last changes fastest.
Arguments:
- features: float32 [16384, 256], P(('blk', 'rep')), may hold values from -6 to 6
- degrees: int32 [16384], P(('blk', 'rep')), may hold values from 8 to 120, as said below
- root_weight: float32 [256, 256], replicated, may hold values from -0.375 to 0.375
- neighbor_weight: float32 [256, 256], replicated, may hold values from -0.375 to 0.375
- bias: float32 [256], replicated, may hold values from -3 to 3
- tile_rows: int32 [16, 16, 16], P('blk', 'rep'), may hold values from 0 to 7
- tile_cols: int32 [16, 16, 16], P('blk', 'rep'), may hold values from 0 to 7
- tile_count: int32 [16, 16], P('blk', 'rep'), may hold values from 1 to 16, as said below
- edge_row: int32 [16, 16, 16, 256], P('blk', 'rep'), may hold values from 0 to 127
- edge_col: int32 [16, 16, 16, 256], P('blk', 'rep'), may hold values from 0 to 127
- edge_weight: int32 [16, 16, 16, 256], P('blk', 'rep'), may hold values from 1 to 4
Outputs:
- activated: float32 [16384, 256], P(('blk', 'rep'))
The draws below stay inside these ranges and needn't reach their ends.
Inputs may be any that keep to these rules, and one draw needn't show every extreme that they name: `degrees`: degrees are whole numbers spread roughly evenly in the logarithm. `tile_count`: every row block and source offset has at least one used slot; some have all 16 used.
All inputs are finite; a program needn't handle non-finite values.
Results may differ from the reference program's by a relative error of at most 0.0003.
Values sent between devices are 32-bit elements; how exact they have to be, the bound alone decides.
No kernel may reach another device: no remote copies, remote signals or barrier semaphores. Data moves between devices by JAX's collectives and lax.ppermute only.
A program may use at most 64 MiB of HBM per device.

```python
import jax
import jax.numpy as jnp
from jax import lax

F = 256
ROWS_DEV = 1024
TCAP = 16
EPT = 256
NODES = 16384
N_BLK = 16


def draw_degrees(key, part):
    key = jax.random.fold_in(key, 11)
    key_exp, key_man = jax.random.split(key)
    exponent = jax.random.randint(key_exp, (NODES,), 3, 7)
    mantissa = jax.random.randint(key_man, (NODES,), 0, 8)
    return jnp.left_shift(8 + mantissa, exponent - 3).astype(jnp.int32)


def draw_tile_count(key, part):
    key = jax.random.fold_in(key, 23)
    raw_count = jax.random.randint(key, (N_BLK, N_BLK), 1, 2 * TCAP + 1)
    return jnp.minimum(raw_count, TCAP).astype(jnp.int32)


def set_ends(drawn, key, low, largest):
    place = [jax.random.randint(jax.random.fold_in(key, axis), (), 0, length) for axis, length in enumerate(drawn.shape)]
    longest = drawn.shape.index(max(drawn.shape))
    next_to = place[:longest] + [(place[longest] + 1) % drawn.shape[longest]] + place[longest + 1:]
    return drawn.at[tuple(place)].set(low).at[tuple(next_to)].set(largest)


def block_scale(own_key, shape, pieces, least, largest):
    factor_of, own = 1.0, jax.random.fold_in(own_key, 6)
    for position, parts in pieces:
        draws = jnp.exp(jax.random.uniform(jax.random.fold_in(own, position), (parts,), jnp.float32, least / len(pieces), largest / len(pieces)))
        factor_of = factor_of * jnp.repeat(draws, shape[position] // parts).reshape([-1 if axis == position else 1 for axis in range(len(shape))])
    return factor_of


def normal_values(rng, dims, deviation, limit, pieces=(), kind=jnp.bfloat16):
    array = jax.random.normal(rng, dims, jnp.float32) * deviation
    if len(pieces) > 0:
        array = block_scale(rng, dims, pieces, -0.22, 0.18) * array
    return jnp.clip(array, min=-limit, max=limit).astype(kind)


def setup_inputs(seed: int = 0) -> dict:
    seeds = jax.random.split(jax.random.key(seed), 12)
    return {
        "features": normal_values(seeds[0], (NODES, F), 1.0, 6.0, ((0, 32),), jnp.float32),
        "degrees": draw_degrees(jax.random.fold_in(seeds[11], 71), 0),
        "root_weight": normal_values(seeds[2], (F, F), F ** -0.5, 0.375, (), jnp.float32),
        "neighbor_weight": normal_values(seeds[3], (F, F), F ** -0.5, 0.375, (), jnp.float32),
        "bias": normal_values(seeds[4], (F,), 0.5, 3.0, (), jnp.float32),
        "tile_rows": set_ends(jax.random.randint(seeds[5], (N_BLK, N_BLK, TCAP), 0, ROWS_DEV // 128), jax.random.fold_in(seeds[5], 1), 0, (ROWS_DEV // 128) - 1).astype(jnp.int32),
        "tile_cols": set_ends(jax.random.randint(seeds[6], (N_BLK, N_BLK, TCAP), 0, ROWS_DEV // 128), jax.random.fold_in(seeds[6], 1), 0, (ROWS_DEV // 128) - 1).astype(jnp.int32),
        "tile_count": draw_tile_count(jax.random.fold_in(seeds[11], 71), 0),
        "edge_row": set_ends(jax.random.randint(seeds[8], (N_BLK, N_BLK, TCAP, EPT), 0, 128), jax.random.fold_in(seeds[8], 1), 0, 127).astype(jnp.int32),
        "edge_col": set_ends(jax.random.randint(seeds[9], (N_BLK, N_BLK, TCAP, EPT), 0, 128), jax.random.fold_in(seeds[9], 1), 0, 127).astype(jnp.int32),
        "edge_weight": set_ends(jax.random.randint(seeds[10], (N_BLK, N_BLK, TCAP, EPT), 1, 5), jax.random.fold_in(seeds[10], 1), 1, 4).astype(jnp.int32),
    }


def reference(features, degrees, root_weight, neighbor_weight, bias, tile_rows, tile_cols, tile_count, edge_row, edge_col, edge_weight):
    highest = lax.Precision.HIGHEST
    scale = lax.rsqrt(degrees.astype(jnp.float32))
    scaled = features * scale[:, None]
    tiles_per = ROWS_DEV // 128
    tiled = scaled.reshape(N_BLK * tiles_per, 128, F)
    offsets = jnp.arange(N_BLK, dtype=jnp.int32)
    slot_ids = jnp.arange(TCAP, dtype=jnp.int32)
    all_slots = N_BLK * TCAP

    def one_block(block_index):
        src_block = (block_index - offsets) % N_BLK
        in_use = (slot_ids[None, :] < tile_count[block_index][:, None]).reshape(all_slots)
        flat_pos = (edge_row[block_index] * 128 + edge_col[block_index]).reshape(all_slots, EPT)
        owners = jnp.broadcast_to(jnp.arange(all_slots, dtype=jnp.int32)[:, None], flat_pos.shape)
        weights_flat = edge_weight[block_index].reshape(all_slots, EPT).astype(jnp.float32)
        tile_mats = jnp.zeros((all_slots, 128 * 128), jnp.float32).at[owners, flat_pos].add(weights_flat)
        tile_mats = tile_mats.reshape(all_slots, 128, 128)
        source_ids = (src_block[:, None] * tiles_per + tile_cols[block_index]).reshape(all_slots).astype(jnp.int32)
        products = jnp.einsum('tab,tbf->taf', tile_mats, tiled[source_ids], precision=highest)
        row_ids = tile_rows[block_index].reshape(all_slots)
        placer = ((row_ids[:, None] == jnp.arange(tiles_per, dtype=jnp.int32)[None, :]) & in_use[:, None]).astype(jnp.float32)
        summed = jnp.einsum('tk,taf->kaf', placer, products, precision=highest)
        return summed.reshape(ROWS_DEV, F)
    aggregate = lax.map(one_block, offsets).reshape(N_BLK * ROWS_DEV, F)
    mixed = aggregate * scale[:, None]
    hidden = jnp.dot(mixed, neighbor_weight, precision=highest) + jnp.dot(features, root_weight, precision=highest) + bias
    return jax.nn.relu(hidden)
```

```python
import functools

import jax
import jax.numpy as jnp
from jax import lax
from jax.experimental import pallas as pl
from jax.experimental.pallas import tpu as pltpu
from jax.sharding import PartitionSpec as P

TILE = 128
UNROLL = 4
SMEM = pl.BlockSpec(memory_space=pltpu.SMEM)
VMEM = pl.BlockSpec(memory_space=pltpu.VMEM)


def bf16_pair(value):
    high = value.astype(jnp.bfloat16)
    low = (value - high.astype(jnp.float32)).astype(jnp.bfloat16)
    return high, low


def tile_matrix(edges, pair, slot, slots, live):
    rows = edges[pair, pl.ds(slot, 1), :]
    cols = edges[pair, pl.ds(slot + slots, 1), :]
    weights = edges[pair, pl.ds(slot + 2 * slots, 1), :]
    weights = jnp.where(live, weights, 0).astype(jnp.float32)
    index = lax.broadcasted_iota(jnp.int32, (TILE, rows.shape[1]), 0)
    row_hot = jnp.where(index == rows, 1.0, 0.0).astype(jnp.bfloat16)
    col_hot = jnp.where(index == cols, weights, 0.0).astype(jnp.bfloat16)
    matrix = lax.dot_general(
        row_hot, col_hot, (((1,), (1,)), ((), ())), preferred_element_type=jnp.float32
    )
    return jnp.concatenate(bf16_pair(matrix), axis=1)


def sum_kernel(sources, chunks, pieces, slots, first, split_out, *refs):
    pairs, place, meta = refs[:3]
    refs = refs[3:]
    blocks, refs = refs[: 2 * sources], refs[2 * sources :]
    count_x = sources * chunks * pieces
    parts, refs = refs[:count_x], refs[count_x:]
    if not first:
        before, refs = refs[:chunks], refs[chunks:]
    if split_out:
        count_out = 4 * chunks
        outs, refs = refs[:count_out], refs[count_out:]
        edges, sides, entries = refs[:3]
        sums = refs[3:]
    else:
        sums, refs = refs[:chunks], refs[chunks:]
        edges, sides, entries = refs
    tiles_here = sides.shape[1]
    tiles_per = sums[0].shape[1] // TILE

    for chunk in range(chunks):
        sums[chunk][...] = jnp.zeros_like(sums[chunk]) if first else before[chunk][...]

    used = jnp.int32(0)
    for number in range(2 * sources):
        edges[number] = blocks[number][0, : 3 * slots]
        pair = pairs[number]
        for slot in range(slots):
            column = meta[pair, slots + slot] - place[0]
            row = lax.rem(meta[pair, slot] + place[1], tiles_per)
            wanted = (slot < meta[pair, 2 * slots]) & (column >= 0) & (column < tiles_here)
            code = ((number * slots + slot) * tiles_here + column) * tiles_per + row
            entries[used] = jnp.where(wanted, code, 0)
            used = used + wanted.astype(jnp.int32)
    for extra in range(UNROLL - 1):
        entries[used + extra] = 0

    for source in range(sources):
        for chunk in range(chunks):
            for piece in range(pieces):
                part = parts[(source * chunks + chunk) * pieces + piece]
                size = min(part.shape[0], TILE)
                for start in range(0, part.shape[0], size):
                    at = piece * part.shape[0] + start
                    high, low = bf16_pair(part[start : start + size, :])
                    for half in range(2):
                        below = half * TILE + at % TILE
                        left = 2 * TILE * chunk
                        sides[source, at // TILE, below : below + size, left : left + TILE] = high
                        sides[source, at // TILE, below : below + size, left + TILE : left + 2 * TILE] = low

    def group(step, carry):
        for lane in range(UNROLL):
            entry = step * UNROLL + lane
            code = entries[entry]
            row = lax.rem(code, tiles_per)
            code = lax.div(code, tiles_per)
            column = lax.rem(code, tiles_here)
            code = lax.div(code, tiles_here)
            slot = lax.rem(code, slots)
            number = lax.div(code, slots)
            matrix = tile_matrix(edges, number, slot, slots, entry < used)
            result = jnp.dot(
                matrix, sides[lax.div(number, 2), column], preferred_element_type=jnp.float32
            )
            at = (lax.rem(number, 2), pl.ds(pl.multiple_of(row * TILE, TILE), TILE), slice(None))
            for chunk in range(chunks):
                left = 2 * TILE * chunk
                sums[chunk][at] += result[:, left : left + TILE] + result[:, left + TILE : left + 2 * TILE]
        return carry

    lax.fori_loop(0, lax.div(used + UNROLL - 1, UNROLL), group, 0)
    if split_out:
        half = sums[0].shape[1] // 2
        for chunk in range(chunks):
            for block in range(2):
                outs[4 * chunk + 2 * block][...] = sums[chunk][block, :half]
                outs[4 * chunk + 2 * block + 1][...] = sums[chunk][block, half:]


def add_sources(pairs, place, meta, edges, parts, before, rows, slots, split_out=False):
    sources, chunks, pieces = len(parts), len(parts[0]), len(parts[0][0])
    flat = [piece for source in parts for chunk in source for piece in chunk]
    width = flat[0].shape[1]
    tiles_here = pieces * flat[0].shape[0] // TILE
    first = before is None
    whole = jax.ShapeDtypeStruct((2, rows, width), jnp.float32)
    quarter = jax.ShapeDtypeStruct((rows // 2, width), jnp.float32)

    def picked(number):
        return pl.BlockSpec(
            (1,) + edges.shape[1:], lambda step, pair_ref, number=number: (pair_ref[number], 0, 0)
        )

    def full(shape):
        return pl.BlockSpec(shape, lambda step, pair_ref: (0,) * len(shape))

    olds = [] if first else list(before)
    outs = [quarter] * (4 * chunks) if split_out else [whole] * chunks
    scratch = [
        pltpu.VMEM((2 * sources, 3 * slots, edges.shape[2]), jnp.int32),
        pltpu.VMEM((sources, tiles_here, 2 * TILE, 2 * TILE * chunks), jnp.bfloat16),
        pltpu.SMEM((2 * sources * slots + UNROLL,), jnp.int32),
    ]
    if split_out:
        scratch += [pltpu.VMEM(whole.shape, jnp.float32)] * chunks
    flops = 2 * sources * 8 * 2 * TILE * TILE * (256 + 4 * TILE * chunks)
    return pl.pallas_call(
        functools.partial(sum_kernel, sources, chunks, pieces, slots, first, split_out),
        grid_spec=pltpu.PrefetchScalarGridSpec(
            num_scalar_prefetch=1,
            grid=(1,),
            in_specs=[SMEM, SMEM]
            + [picked(number) for number in range(2 * sources)]
            + [full(part.shape) for part in flat]
            + [full(old.shape) for old in olds],
            out_specs=[full(out.shape) for out in outs],
            scratch_shapes=scratch,
        ),
        out_shape=outs,
        compiler_params=pltpu.CompilerParams(vmem_limit_bytes=24 << 20),
        cost_estimate=pl.CostEstimate(flops=flops, bytes_accessed=4 << 20, transcendentals=0),
    )(pairs, place, meta, *([edges] * (2 * sources)), *flat, *olds)


def on_device(
    features,
    degrees,
    root_weight,
    neighbor_weight,
    bias,
    tile_rows,
    tile_cols,
    tile_count,
    edge_row,
    edge_col,
    edge_weight,
):
    highest = lax.Precision.HIGHEST
    groups, blocks = lax.axis_size("rep"), lax.axis_size("blk")
    lanes = blocks // 2
    layers = lanes // 2
    arc, slots, listed = edge_row.shape[1:]
    per = arc // 2
    shard, width = features.shape
    rows = shard * groups
    chunks, pieces = width // TILE, 2
    block, replica = lax.axis_index("blk"), lax.axis_index("rep")
    chip, core = block // 2, block % 2

    def chip_at(position):
        return 2 * position if position < layers else 2 * (lanes - 1 - position) + 1

    def ring(value, step):
        pairs = [
            (2 * chip_at(p) + c, 2 * chip_at((p + step) % lanes) + c) for p in range(lanes) for c in range(2)
        ]
        return lax.ppermute(value, "blk", pairs)

    def core_swap(value):
        return lax.ppermute(value, "blk", [(b, b ^ 1) for b in range(blocks)])

    def rep_swap(value):
        return lax.ppermute(value, "rep", [(0, 1), (1, 0)])

    scale = lax.rsqrt(degrees.astype(jnp.float32))
    scaled = features * scale[:, None]
    cut = shard // pieces
    own = [
        [scaled[h * cut : (h + 1) * cut, f * TILE : (f + 1) * TILE] for h in range(pieces)] for f in range(chunks)
    ]

    def bundle(start):
        lists = [array[0, start::2] for array in (edge_row, edge_col, edge_weight)]
        head = jnp.concatenate(
            [tile_rows[0, start::2], tile_cols[0, start::2], tile_count[0, start::2, None]], axis=1
        )
        head = jnp.pad(head, ((0, 0), (0, listed - head.shape[1])))[:, None]
        head = jnp.pad(head, ((0, 0), (0, 7), (0, 0)))
        return jnp.concatenate(lists + [head], axis=1)

    own_lists = bundle(0)
    sibling_lists = core_swap(bundle(1))
    if groups == 2:
        gathered = [own_lists, rep_swap(own_lists), sibling_lists, rep_swap(sibling_lists)]
    else:
        gathered = [lax.all_gather(lists, "rep", axis=0, tiled=True) for lists in (own_lists, sibling_lists)]
    edges = jnp.concatenate(gathered, axis=0)
    meta = edges[:, 3 * slots, :TILE]

    def list_place(offset):
        group = offset // per
        group = group ^ replica if groups == 2 else group
        return group * per + offset % per

    position = jnp.where(chip % 2 == 0, chip // 2, lanes - 1 - chip // 2)

    def pairs_of(distances):
        places = []
        for distance in distances:
            there = (position + distance + lanes) % lanes
            source = jnp.where(there < layers, 2 * there, 2 * (lanes - 1 - there) + 1)
            places.append(list_place((chip - source + lanes) % lanes))
            places.append(groups * per + list_place((chip - source - core + lanes) % lanes))
        return jnp.stack(places).astype(jnp.int32)

    tiles_per = rows // TILE
    tiles_here = shard // TILE
    rotation = (tiles_per - replica * tiles_here) if groups == 2 else 0 * replica
    place = jnp.stack([replica * tiles_here, rotation]).astype(jnp.int32)
    add = functools.partial(add_sources, rows=rows, slots=slots)

    root = jnp.dot(features, root_weight, precision=highest) + bias

    up, down = own, own
    totals = None
    for step in range(1, lanes // 2 + 1):
        last = step == lanes // 2
        up = [[ring(v, 1) if h == 0 or not last else None for h, v in enumerate(f)] for f in up]
        down = [[ring(v, -1) if h == 1 or not last else None for h, v in enumerate(f)] for f in down]
        if step == 1:
            totals = add(pairs_of([0]), place, meta, edges, [own], None)
        if not last:
            totals = add(pairs_of([-step, step]), place, meta, edges, [up, down], totals)
    pairs = pairs_of([lanes // 2])
    hidden = root
    for f in range(chunks):
        ends = add(pairs, place, meta, edges, [[[up[f][0], down[f][1]]]], [totals[f]], split_out=True)
        own_mine, own_other, sibling_mine, sibling_other = ends
        if groups == 2:
            other = rep_swap(own_other + core_swap(sibling_other))
            share = own_mine + core_swap(sibling_mine) + other
        else:
            mine = jnp.concatenate([own_mine, own_other], 0) + core_swap(
                jnp.concatenate([sibling_mine, sibling_other], 0)
            )
            share = lax.psum_scatter(mine, "rep", scatter_dimension=0, tiled=True)
        mixed = share * scale[:, None]
        hidden = hidden + jnp.dot(mixed, neighbor_weight[f * TILE : (f + 1) * TILE], precision=highest)
    return jax.nn.relu(hidden)


def solution(mesh):
    placed = (
        P(("blk", "rep"), None),
        P(("blk", "rep")),
        P(),
        P(),
        P(),
        P("blk", "rep", None),
        P("blk", "rep", None),
        P("blk", "rep"),
        P("blk", "rep", None, None),
        P("blk", "rep", None, None),
        P("blk", "rep", None, None),
    )
    return jax.shard_map(
        on_device, mesh=mesh, in_specs=placed, out_specs=P(("blk", "rep"), None), check_vma=False
    )
```

```python
import functools

import jax
import jax.numpy as jnp
from jax import lax
from jax.experimental import pallas as pl
from jax.experimental.pallas import tpu as pltpu
from jax.sharding import PartitionSpec as P

TILE = 128
UNROLL = 8
SMEM = pl.BlockSpec(memory_space=pltpu.SMEM)
VMEM = pl.BlockSpec(memory_space=pltpu.VMEM)


def bf16_pair(value):
    high = value.astype(jnp.bfloat16)
    low = (value - high.astype(jnp.float32)).astype(jnp.bfloat16)
    return high, low


def tile_matrix(edges, pair, slot, slots, live):
    rows = edges[pair, pl.ds(slot, 1), :]
    cols = edges[pair, pl.ds(slot + slots, 1), :]
    weights = edges[pair, pl.ds(slot + 2 * slots, 1), :]
    weights = jnp.where(live, weights, 0).astype(jnp.float32)
    index = lax.broadcasted_iota(jnp.int32, (TILE, rows.shape[1]), 0)
    row_hot = jnp.where(index == rows, 1.0, 0.0).astype(jnp.bfloat16)
    col_hot = jnp.where(index == cols, weights, 0.0).astype(jnp.bfloat16)
    matrix = lax.dot_general(
        row_hot, col_hot, (((1,), (1,)), ((), ())), preferred_element_type=jnp.float32
    )
    return jnp.concatenate(bf16_pair(matrix), axis=1)


def sum_kernel(sources, chunks, slots, first, last, *refs):
    pairs, place, meta, edges = refs[:4]
    refs = refs[4:]
    parts, refs = refs[: sources * chunks], refs[sources * chunks :]
    if not first:
        before, refs = refs[:chunks], refs[chunks:]
    if last:
        outs, sides, entries = refs[: 2 * chunks], refs[2 * chunks], refs[2 * chunks + 1]
        sums = refs[2 * chunks + 2 :]
    else:
        sums, sides, entries = refs[:chunks], refs[chunks], refs[chunks + 1]
    tiles_here = sides.shape[1]
    tiles_per = sums[0].shape[1] // TILE

    for chunk in range(chunks):
        if first:
            sums[chunk][...] = jnp.zeros_like(sums[chunk])
        else:
            sums[chunk][...] = before[chunk][...]

    used = jnp.int32(0)
    for number in range(2 * sources):
        pair = pairs[number]
        for slot in range(slots):
            column = meta[pair, slots + slot] - place[0]
            row = (meta[pair, slot] + place[1]) & (tiles_per - 1)
            wanted = (slot < meta[pair, 2 * slots]) & (column >= 0) & (column < tiles_here)
            code = ((number * slots + slot) * tiles_here + column) * tiles_per + row
            entries[used] = jnp.where(wanted, code, 0)
            used = used + wanted.astype(jnp.int32)
    for extra in range(UNROLL - 1):
        entries[used + extra] = 0

    for source in range(sources):
        for chunk in range(chunks):
            part = parts[source * chunks + chunk]
            left = 2 * TILE * chunk
            for tile in range(tiles_here):
                high, low = bf16_pair(part[tile * TILE : (tile + 1) * TILE, :])
                for half in range(2):
                    below = half * TILE
                    sides[source, tile, below : below + TILE, left : left + TILE] = high
                    sides[source, tile, below : below + TILE, left + TILE : left + 2 * TILE] = low

    def group(step, carry):
        todo = []
        for lane in range(UNROLL):
            entry = step * UNROLL + lane
            code = entries[entry]
            row = code & (tiles_per - 1)
            code = lax.div(code, tiles_per)
            column = lax.rem(code, tiles_here)
            code = lax.div(code, tiles_here)
            slot = lax.rem(code, slots)
            number = lax.div(code, slots)
            matrix = tile_matrix(edges, pairs[number], slot, slots, entry < used)
            todo.append((matrix, number, column, row))
        results = [
            jnp.dot(matrix, sides[lax.div(number, 2), column], preferred_element_type=jnp.float32)
            for matrix, number, column, _ in todo
        ]
        for (_, number, _, row), result in zip(todo, results):
            at = (lax.rem(number, 2), pl.ds(pl.multiple_of(row * TILE, TILE), TILE), slice(None))
            for chunk in range(chunks):
                left = 2 * TILE * chunk
                sums[chunk][at] += result[:, left : left + TILE] + result[:, left + TILE : left + 2 * TILE]
        return carry

    lax.fori_loop(0, lax.div(used + UNROLL - 1, UNROLL), group, 0)
    if last:
        for chunk in range(chunks):
            for block in range(2):
                outs[2 * chunk + block][...] = sums[chunk][block]


def add_sources(pairs, place, meta, edges, parts, before, rows, slots, last=False):
    sources, chunks = len(parts), len(parts[0])
    flat = [chunk for source in parts for chunk in source]
    here, width = flat[0].shape
    first = before is None
    whole = jax.ShapeDtypeStruct((2, rows, width), jnp.float32)
    block = jax.ShapeDtypeStruct((rows, width), jnp.float32)
    olds = [] if first else list(before)
    outs = [block] * (2 * chunks) if last else [whole] * chunks
    scratch = [
        pltpu.VMEM((sources, here // TILE, 2 * TILE, 2 * TILE * chunks), jnp.bfloat16),
        pltpu.SMEM((2 * sources * slots + UNROLL,), jnp.int32),
    ]
    if last:
        scratch += [pltpu.VMEM(whole.shape, jnp.float32)] * chunks
    flops = 2 * sources * 8 * 2 * TILE * TILE * (256 + 4 * TILE * chunks)
    return pl.pallas_call(
        functools.partial(sum_kernel, sources, chunks, slots, first, last),
        in_specs=[SMEM] * 3 + [VMEM] * (1 + len(flat) + len(olds)),
        out_specs=[VMEM] * len(outs),
        out_shape=outs,
        scratch_shapes=scratch,
        compiler_params=pltpu.CompilerParams(vmem_limit_bytes=24 << 20),
        cost_estimate=pl.CostEstimate(flops=flops, bytes_accessed=4 << 20, transcendentals=0),
    )(pairs, place, meta, edges, *flat, *olds)


def on_device(
    features,
    degrees,
    root_weight,
    neighbor_weight,
    bias,
    tile_rows,
    tile_cols,
    tile_count,
    edge_row,
    edge_col,
    edge_weight,
):
    highest = lax.Precision.HIGHEST
    groups, blocks = lax.axis_size("rep"), lax.axis_size("blk")
    lanes = blocks // 2
    layers = lanes // 2
    arc, slots, listed = edge_row.shape[1:]
    per = arc // 2
    shard, width = features.shape
    rows = shard * groups
    chunks = width // TILE
    block, replica = lax.axis_index("blk"), lax.axis_index("rep")
    chip, core = block // 2, block % 2

    def chip_at(position):
        return 2 * position if position < layers else 2 * (lanes - 1 - position) + 1

    def ring(value, step):
        pairs = [
            (2 * chip_at(p) + c, 2 * chip_at((p + step) % lanes) + c) for p in range(lanes) for c in range(2)
        ]
        return lax.ppermute(value, "blk", pairs)

    def core_swap(value):
        return lax.ppermute(value, "blk", [(b, b ^ 1) for b in range(blocks)])

    def rep_swap(value):
        return lax.ppermute(value, "rep", [(0, 1), (1, 0)])

    scale = lax.rsqrt(degrees.astype(jnp.float32))
    scaled = features * scale[:, None]
    own = [scaled[:, f * TILE : (f + 1) * TILE] for f in range(chunks)]

    def bundle(start):
        lists = [array[0, start::2] for array in (edge_row, edge_col, edge_weight)]
        head = jnp.concatenate(
            [tile_rows[0, start::2], tile_cols[0, start::2], tile_count[0, start::2, None]], axis=1
        )
        head = jnp.pad(head, ((0, 0), (0, listed - head.shape[1])))[:, None]
        head = jnp.pad(head, ((0, 0), (0, 7), (0, 0)))
        return jnp.concatenate(lists + [head], axis=1)

    own_lists = bundle(0)
    sibling_lists = core_swap(bundle(1))
    lists = jnp.concatenate([own_lists, sibling_lists], axis=0)
    if groups == 2:
        edges = jnp.concatenate([lists, rep_swap(lists)], axis=0)
    else:
        edges = lax.all_gather(lists, "rep", axis=0, tiled=True)
    meta = edges[:, 3 * slots, :TILE]

    def list_place(offset, which):
        group = offset // per
        group = group ^ replica if groups == 2 else group
        return (2 * group + which) * per + offset % per

    position = jnp.where(chip % 2 == 0, chip // 2, lanes - 1 - chip // 2)

    def pairs_of(distances):
        places = []
        for distance in distances:
            there = (position + distance + lanes) % lanes
            source = jnp.where(there < layers, 2 * there, 2 * (lanes - 1 - there) + 1)
            places.append(list_place((chip - source + lanes) % lanes, 0))
            places.append(list_place((chip - source - core + lanes) % lanes, 1))
        return jnp.stack(places).astype(jnp.int32)

    tiles_per = rows // TILE
    tiles_here = shard // TILE
    rotation = (tiles_per - replica * tiles_here) if groups == 2 else 0 * replica
    place = jnp.stack([replica * tiles_here, rotation]).astype(jnp.int32)
    add = functools.partial(add_sources, rows=rows, slots=slots)

    root = jnp.dot(features, root_weight, precision=highest) + bias

    up, down = own, own
    totals = None
    for step in range(1, lanes // 2 + 1):
        last = step == lanes // 2
        up = [ring(v, 1) if f % 2 == 0 or not last else None for f, v in enumerate(up)]
        down = [ring(v, -1) if f % 2 == 1 or not last else None for f, v in enumerate(down)]
        if step == 1:
            totals = add(pairs_of([0]), place, meta, edges, [own], None)
        if not last:
            totals = add(pairs_of([-step, step]), place, meta, edges, [up, down], totals)
    pairs = pairs_of([lanes // 2])
    hidden = root
    for f in range(chunks):
        end = up[f] if f % 2 == 0 else down[f]
        own_sum, sibling_sum = add(pairs, place, meta, edges, [[end]], [totals[f]], last=True)
        swapped = core_swap(sibling_sum)
        if groups == 2:
            other = rep_swap(own_sum[shard:] + swapped[shard:])
            share = own_sum[:shard] + swapped[:shard] + other
        else:
            share = lax.psum_scatter(own_sum + swapped, "rep", scatter_dimension=0, tiled=True)
        mixed = share * scale[:, None]
        hidden = hidden + jnp.dot(mixed, neighbor_weight[f * TILE : (f + 1) * TILE], precision=highest)
    return jax.nn.relu(hidden)


def solution(mesh):
    placed = (
        P(("blk", "rep"), None),
        P(("blk", "rep")),
        P(),
        P(),
        P(),
        P("blk", "rep", None),
        P("blk", "rep", None),
        P("blk", "rep"),
        P("blk", "rep", None, None),
        P("blk", "rep", None, None),
        P("blk", "rep", None, None),
    )
    return jax.shard_map(
        on_device, mesh=mesh, in_specs=placed, out_specs=P(("blk", "rep"), None), check_vma=False
    )
```

```python
import functools

import jax
import jax.numpy as jnp
from jax import lax
from jax.experimental import pallas as pl
from jax.experimental.pallas import tpu as pltpu
from jax.sharding import PartitionSpec as P

TILE = 128
UNROLL = 8
SMEM = pl.BlockSpec(memory_space=pltpu.SMEM)
VMEM = pl.BlockSpec(memory_space=pltpu.VMEM)


def bf16_pair(value):
    high = value.astype(jnp.bfloat16)
    low = (value - high.astype(jnp.float32)).astype(jnp.bfloat16)
    return high, low


def tile_matrix(edges, pair, slot, slots, live):
    rows = edges[pair, pl.ds(slot, 1), :]
    cols = edges[pair, pl.ds(slot + slots, 1), :]
    weights = edges[pair, pl.ds(slot + 2 * slots, 1), :]
    weights = jnp.where(live, weights, 0).astype(jnp.float32)
    index = lax.broadcasted_iota(jnp.int32, (TILE, rows.shape[1]), 0)
    row_hot = jnp.where(index == rows, 1.0, 0.0).astype(jnp.bfloat16)
    col_hot = jnp.where(index == cols, weights, 0.0).astype(jnp.bfloat16)
    matrix = lax.dot_general(
        row_hot, col_hot, (((1,), (1,)), ((), ())), preferred_element_type=jnp.float32
    )
    return jnp.concatenate(bf16_pair(matrix), axis=1)


def sum_kernel(sources, chunks, pieces, slots, first, last, *refs):
    pairs, place, meta, edges = refs[:4]
    refs = refs[4:]
    count = sources * chunks * pieces
    parts, refs = refs[:count], refs[count:]
    if not first:
        before, refs = refs[:chunks], refs[chunks:]
    if last:
        outs, sides, entries = refs[: 2 * chunks], refs[2 * chunks], refs[2 * chunks + 1]
        sums = refs[2 * chunks + 2 :]
    else:
        sums, sides, entries = refs[:chunks], refs[chunks], refs[chunks + 1]
    tiles_here = sides.shape[1]
    tiles_per = sums[0].shape[1] // TILE

    for chunk in range(chunks):
        if first:
            sums[chunk][...] = jnp.zeros_like(sums[chunk])
        elif last:
            sums[chunk][...] = before[chunk][...]

    used = jnp.int32(0)
    for number in range(2 * sources):
        pair = pairs[number]
        for slot in range(slots):
            column = meta[pair, slots + slot] - place[0]
            row = (meta[pair, slot] + place[1]) & (tiles_per - 1)
            wanted = (slot < meta[pair, 2 * slots]) & (column >= 0) & (column < tiles_here)
            code = ((number * slots + slot) * tiles_here + column) * tiles_per + row
            entries[used] = jnp.where(wanted, code, 0)
            used = used + wanted.astype(jnp.int32)
    for extra in range(UNROLL - 1):
        entries[used + extra] = 0

    for source in range(sources):
        for chunk in range(chunks):
            left = 2 * TILE * chunk
            for piece in range(pieces):
                part = parts[(source * chunks + chunk) * pieces + piece]
                size = min(part.shape[0], TILE)
                for start in range(0, part.shape[0], size):
                    at = piece * part.shape[0] + start
                    high, low = bf16_pair(part[start : start + size, :])
                    for half in range(2):
                        below = half * TILE + at % TILE
                        sides[source, at // TILE, below : below + size, left : left + TILE] = high
                        sides[source, at // TILE, below : below + size, left + TILE : left + 2 * TILE] = low

    def group(step, carry):
        todo = []
        for lane in range(UNROLL):
            entry = step * UNROLL + lane
            code = entries[entry]
            row = code & (tiles_per - 1)
            code = lax.div(code, tiles_per)
            column = lax.rem(code, tiles_here)
            code = lax.div(code, tiles_here)
            slot = lax.rem(code, slots)
            number = lax.div(code, slots)
            matrix = tile_matrix(edges, pairs[number], slot, slots, entry < used)
            todo.append((matrix, number, column, row))
        results = [
            jnp.dot(matrix, sides[lax.div(number, 2), column], preferred_element_type=jnp.float32)
            for matrix, number, column, _ in todo
        ]
        for (_, number, _, row), result in zip(todo, results):
            at = (lax.rem(number, 2), pl.ds(pl.multiple_of(row * TILE, TILE), TILE), slice(None))
            for chunk in range(chunks):
                left = 2 * TILE * chunk
                sums[chunk][at] += result[:, left : left + TILE] + result[:, left + TILE : left + 2 * TILE]
        return carry

    lax.fori_loop(0, lax.div(used + UNROLL - 1, UNROLL), group, 0)
    if last:
        for chunk in range(chunks):
            for block in range(2):
                outs[2 * chunk + block][...] = sums[chunk][block]


def add_sources(pairs, place, meta, edges, parts, before, rows, slots, last=False):
    sources, chunks, pieces = len(parts), len(parts[0]), len(parts[0][0])
    flat = [piece for source in parts for chunk in source for piece in chunk]
    here, width = pieces * flat[0].shape[0], flat[0].shape[1]
    first = before is None
    whole = jax.ShapeDtypeStruct((2, rows, width), jnp.float32)
    block = jax.ShapeDtypeStruct((rows, width), jnp.float32)
    olds = [] if first else list(before)
    outs = [block] * (2 * chunks) if last else [pltpu.VMEM(whole.shape, whole.dtype)] * chunks
    scratch = [
        pltpu.VMEM((sources, here // TILE, 2 * TILE, 2 * TILE * chunks), jnp.bfloat16),
        pltpu.SMEM((2 * sources * slots + UNROLL,), jnp.int32),
    ]
    aliases = {}
    if last:
        scratch += [pltpu.VMEM(whole.shape, jnp.float32)] * chunks
    elif not first:
        olds = [pltpu.with_memory_space_constraint(old, pltpu.VMEM) for old in olds]
        aliases = {4 + len(flat) + chunk: chunk for chunk in range(chunks)}
    flops = 1_000_000_000 * (1 + sources * chunks)
    return pl.pallas_call(
        functools.partial(sum_kernel, sources, chunks, pieces, slots, first, last),
        in_specs=[SMEM] * 3 + [VMEM] * (1 + len(flat) + len(olds)),
        out_specs=[VMEM] * len(outs),
        out_shape=outs,
        scratch_shapes=scratch,
        input_output_aliases=aliases,
        compiler_params=pltpu.CompilerParams(vmem_limit_bytes=24 << 20),
        cost_estimate=pl.CostEstimate(flops=flops, bytes_accessed=1 << 20, transcendentals=0),
    )(pairs, place, meta, edges, *flat, *olds)


def on_device(
    features,
    degrees,
    root_weight,
    neighbor_weight,
    bias,
    tile_rows,
    tile_cols,
    tile_count,
    edge_row,
    edge_col,
    edge_weight,
):
    highest = lax.Precision.HIGHEST
    groups, blocks = lax.axis_size("rep"), lax.axis_size("blk")
    lanes = blocks // 2
    layers = lanes // 2
    arc, slots, listed = edge_row.shape[1:]
    per = arc // 2
    shard, width = features.shape
    rows = shard * groups
    chunks = width // TILE
    block, replica = lax.axis_index("blk"), lax.axis_index("rep")
    chip, core = block // 2, block % 2

    def chip_at(position):
        return 2 * position if position < layers else 2 * (lanes - 1 - position) + 1

    def ring(value, step):
        pairs = [
            (2 * chip_at(p) + c, 2 * chip_at((p + step) % lanes) + c) for p in range(lanes) for c in range(2)
        ]
        return lax.ppermute(value, "blk", pairs)

    def core_swap(value):
        return lax.ppermute(value, "blk", [(b, b ^ 1) for b in range(blocks)])

    def rep_swap(value):
        return lax.ppermute(value, "rep", [(0, 1), (1, 0)])

    scale = lax.rsqrt(degrees.astype(jnp.float32))
    scaled = features * scale[:, None]
    own = [scaled[:, f * TILE : (f + 1) * TILE] for f in range(chunks)]

    def bundle(start):
        lists = [array[0, start::2] for array in (edge_row, edge_col, edge_weight)]
        head = jnp.concatenate(
            [tile_rows[0, start::2], tile_cols[0, start::2], tile_count[0, start::2, None]], axis=1
        )
        head = jnp.pad(head, ((0, 0), (0, listed - head.shape[1])))[:, None]
        head = jnp.pad(head, ((0, 0), (0, 7), (0, 0)))
        return jnp.concatenate(lists + [head], axis=1)

    own_lists, others_lists = bundle(0), bundle(1)
    if groups == 2:
        own_far = rep_swap(own_lists)
        sibling_lists = core_swap(others_lists)
        edges = jnp.concatenate([own_lists, own_far, sibling_lists, rep_swap(sibling_lists)], axis=0)
    else:
        lists = jnp.concatenate([own_lists, core_swap(others_lists)], axis=1)
        lists = lax.all_gather(lists, "rep", axis=0, tiled=True)
        edges = jnp.concatenate([lists[:, : own_lists.shape[1]], lists[:, own_lists.shape[1] :]], axis=0)
    meta = edges[:, 3 * slots, :TILE]

    def list_place(offset, which):
        group = offset // per
        group = group ^ replica if groups == 2 else group
        return (which * groups + group) * per + offset % per

    position = jnp.where(chip % 2 == 0, chip // 2, lanes - 1 - chip // 2)

    def pairs_of(distances):
        places = []
        for distance in distances:
            there = (position + distance + lanes) % lanes
            source = jnp.where(there < layers, 2 * there, 2 * (lanes - 1 - there) + 1)
            places.append(list_place((chip - source + lanes) % lanes, 0))
            places.append(list_place((chip - source - core + lanes) % lanes, 1))
        return jnp.stack(places).astype(jnp.int32)

    tiles_per = rows // TILE
    tiles_here = shard // TILE
    rotation = (tiles_per - replica * tiles_here) if groups == 2 else 0 * replica
    place = jnp.stack([replica * tiles_here, rotation]).astype(jnp.int32)
    add = functools.partial(add_sources, rows=rows, slots=slots)

    root = jnp.dot(features, root_weight, precision=highest) + bias

    half = shard // 2
    up, down = own, own
    totals = add(pairs_of([0]), place, meta, edges, [[[v] for v in own]], None)
    for step in range(1, lanes // 2):
        up, down = [ring(v, 1) for v in up], [ring(v, -1) for v in down]
        if step == lanes // 2 - 1:
            for f in range(chunks):
                up[f], down[f], totals = lax.optimization_barrier((up[f], down[f], totals))
        parts = [[[v] for v in up], [[v] for v in down]]
        totals = add(pairs_of([-step, step]), place, meta, edges, parts, totals)
    ends = [[ring(up[f][:half], 1), ring(down[f][half:], -1)] for f in range(chunks)]
    pairs = pairs_of([lanes // 2])
    hidden = root
    for f in range(chunks):
        own_sum, sibling_sum = add(pairs, place, meta, edges, [[ends[f]]], [totals[f]], last=True)
        swapped = core_swap(sibling_sum)
        if groups == 2:
            other = rep_swap(own_sum[shard:] + swapped[shard:])
            share = own_sum[:shard] + swapped[:shard] + other
        else:
            share = lax.psum_scatter(own_sum + swapped, "rep", scatter_dimension=0, tiled=True)
        mixed = share * scale[:, None]
        hidden = hidden + jnp.dot(mixed, neighbor_weight[f * TILE : (f + 1) * TILE], precision=highest)
    return jax.nn.relu(hidden)


def solution(mesh):
    placed = (
        P(("blk", "rep"), None),
        P(("blk", "rep")),
        P(),
        P(),
        P(),
        P("blk", "rep", None),
        P("blk", "rep", None),
        P("blk", "rep"),
        P("blk", "rep", None, None),
        P("blk", "rep", None, None),
        P("blk", "rep", None, None),
    )
    return jax.shard_map(
        on_device, mesh=mesh, in_specs=placed, out_specs=P(("blk", "rep"), None), check_vma=False
    )
```

```python
import functools

import jax
import jax.numpy as jnp
from jax import lax
from jax.experimental import pallas as pl
from jax.experimental.pallas import tpu as pltpu
from jax.sharding import PartitionSpec as P

TILE = 128
UNROLL = 8
SMEM = pl.BlockSpec(memory_space=pltpu.SMEM)
VMEM = pl.BlockSpec(memory_space=pltpu.VMEM)


def bf16_pair(value):
    high = value.astype(jnp.bfloat16)
    low = (value - high.astype(jnp.float32)).astype(jnp.bfloat16)
    return high, low


def tile_matrix(edges, pair, slot, slots, live):
    rows = edges[pair, pl.ds(slot, 1), :]
    cols = edges[pair, pl.ds(slot + slots, 1), :]
    weights = edges[pair, pl.ds(slot + 2 * slots, 1), :]
    weights = jnp.where(live, weights, 0).astype(jnp.float32)
    index = lax.broadcasted_iota(jnp.int32, (TILE, rows.shape[1]), 0)
    row_hot = jnp.where(index == rows, 1.0, 0.0).astype(jnp.bfloat16)
    col_hot = jnp.where(index == cols, weights, 0.0).astype(jnp.bfloat16)
    matrix = lax.dot_general(
        row_hot, col_hot, (((1,), (1,)), ((), ())), preferred_element_type=jnp.float32
    )
    return jnp.concatenate(bf16_pair(matrix), axis=1)


def sum_kernel(sources, chunks, pieces, slots, first, last, *refs):
    pairs, place, meta, edges = refs[:4]
    refs = refs[4:]
    count = sources * chunks * pieces
    parts, refs = refs[:count], refs[count:]
    if not first:
        before, refs = refs[:chunks], refs[chunks:]
    if last:
        outs, sides, entries = refs[: 2 * chunks], refs[2 * chunks], refs[2 * chunks + 1]
        sums = refs[2 * chunks + 2 :]
    else:
        sums, sides, entries = refs[:chunks], refs[chunks], refs[chunks + 1]
    tiles_here = sides.shape[1]
    tiles_per = sums[0].shape[1] // TILE

    for chunk in range(chunks):
        if first:
            sums[chunk][...] = jnp.zeros_like(sums[chunk])
        elif last:
            sums[chunk][...] = before[chunk][...]

    used = jnp.int32(0)
    for number in range(2 * sources):
        pair = pairs[number]
        for slot in range(slots):
            column = meta[pair, slots + slot] - place[0]
            row = (meta[pair, slot] + place[1]) & (tiles_per - 1)
            wanted = (slot < meta[pair, 2 * slots]) & (column >= 0) & (column < tiles_here)
            code = ((number * slots + slot) * tiles_here + column) * tiles_per + row
            entries[used] = jnp.where(wanted, code, 0)
            used = used + wanted.astype(jnp.int32)
    for extra in range(UNROLL - 1):
        entries[used + extra] = 0

    for source in range(sources):
        for chunk in range(chunks):
            left = 2 * TILE * chunk
            for piece in range(pieces):
                part = parts[(source * chunks + chunk) * pieces + piece]
                size = min(part.shape[0], TILE)
                for start in range(0, part.shape[0], size):
                    at = piece * part.shape[0] + start
                    high, low = bf16_pair(part[start : start + size, :])
                    for half in range(2):
                        below = half * TILE + at % TILE
                        sides[source, at // TILE, below : below + size, left : left + TILE] = high
                        sides[source, at // TILE, below : below + size, left + TILE : left + 2 * TILE] = low

    def group(step, carry):
        todo = []
        for lane in range(UNROLL):
            entry = step * UNROLL + lane
            code = entries[entry]
            row = code & (tiles_per - 1)
            code = lax.div(code, tiles_per)
            column = lax.rem(code, tiles_here)
            code = lax.div(code, tiles_here)
            slot = lax.rem(code, slots)
            number = lax.div(code, slots)
            matrix = tile_matrix(edges, pairs[number], slot, slots, entry < used)
            todo.append((matrix, number, column, row))
        results = [
            jnp.dot(matrix, sides[lax.div(number, 2), column], preferred_element_type=jnp.float32)
            for matrix, number, column, _ in todo
        ]
        for (_, number, _, row), result in zip(todo, results):
            at = (lax.rem(number, 2), pl.ds(pl.multiple_of(row * TILE, TILE), TILE), slice(None))
            for chunk in range(chunks):
                left = 2 * TILE * chunk
                sums[chunk][at] += result[:, left : left + TILE] + result[:, left + TILE : left + 2 * TILE]
        return carry

    lax.fori_loop(0, lax.div(used + UNROLL - 1, UNROLL), group, 0)
    if last:
        for chunk in range(chunks):
            for block in range(2):
                outs[2 * chunk + block][...] = sums[chunk][block]


def add_sources(pairs, place, meta, edges, parts, before, rows, slots, last=False):
    sources, chunks, pieces = len(parts), len(parts[0]), len(parts[0][0])
    flat = [piece for source in parts for chunk in source for piece in chunk]
    here, width = pieces * flat[0].shape[0], flat[0].shape[1]
    first = before is None
    whole = jax.ShapeDtypeStruct((2, rows, width), jnp.float32)
    block = jax.ShapeDtypeStruct((rows, width), jnp.float32)
    olds = [] if first else list(before)
    outs = [block] * (2 * chunks) if last else [pltpu.VMEM(whole.shape, whole.dtype)] * chunks
    scratch = [
        pltpu.VMEM((sources, here // TILE, 2 * TILE, 2 * TILE * chunks), jnp.bfloat16),
        pltpu.SMEM((2 * sources * slots + UNROLL,), jnp.int32),
    ]
    aliases = {}
    if last:
        scratch += [pltpu.VMEM(whole.shape, jnp.float32)] * chunks
    elif not first:
        olds = [pltpu.with_memory_space_constraint(old, pltpu.VMEM) for old in olds]
        aliases = {4 + len(flat) + chunk: chunk for chunk in range(chunks)}
    flops = 1_000_000_000 * (1 + sources * chunks)
    return pl.pallas_call(
        functools.partial(sum_kernel, sources, chunks, pieces, slots, first, last),
        in_specs=[SMEM] * 3 + [VMEM] * (1 + len(flat) + len(olds)),
        out_specs=[VMEM] * len(outs),
        out_shape=outs,
        scratch_shapes=scratch,
        input_output_aliases=aliases,
        compiler_params=pltpu.CompilerParams(vmem_limit_bytes=24 << 20),
        cost_estimate=pl.CostEstimate(flops=flops, bytes_accessed=1 << 20, transcendentals=0),
    )(pairs, place, meta, edges, *flat, *olds)


def on_device(
    features,
    degrees,
    root_weight,
    neighbor_weight,
    bias,
    tile_rows,
    tile_cols,
    tile_count,
    edge_row,
    edge_col,
    edge_weight,
):
    highest = lax.Precision.HIGHEST
    groups, blocks = lax.axis_size("rep"), lax.axis_size("blk")
    lanes = blocks // 2
    layers = lanes // 2
    arc, slots, listed = edge_row.shape[1:]
    per = arc // 2
    shard, width = features.shape
    rows = shard * groups
    chunks = width // TILE
    block, replica = lax.axis_index("blk"), lax.axis_index("rep")
    chip, core = block // 2, block % 2

    def chip_at(position):
        return 2 * position if position < layers else 2 * (lanes - 1 - position) + 1

    def ring(value, step):
        pairs = [
            (2 * chip_at(p) + c, 2 * chip_at((p + step) % lanes) + c) for p in range(lanes) for c in range(2)
        ]
        return lax.ppermute(value, "blk", pairs)

    def core_swap(value):
        return lax.ppermute(value, "blk", [(b, b ^ 1) for b in range(blocks)])

    def rep_swap(value):
        return lax.ppermute(value, "rep", [(0, 1), (1, 0)])

    scale = lax.rsqrt(degrees.astype(jnp.float32))
    scaled = features * scale[:, None]
    own = [scaled[:, f * TILE : (f + 1) * TILE] for f in range(chunks)]

    def bundle(start):
        lists = [array[0, start::2] for array in (edge_row, edge_col, edge_weight)]
        head = jnp.concatenate(
            [tile_rows[0, start::2], tile_cols[0, start::2], tile_count[0, start::2, None]], axis=1
        )
        head = jnp.pad(head, ((0, 0), (0, listed - head.shape[1])))[:, None]
        head = jnp.pad(head, ((0, 0), (0, 7), (0, 0)))
        return jnp.concatenate(lists + [head], axis=1)

    lists = jnp.concatenate([bundle(0), core_swap(bundle(1))], axis=0)
    if groups == 2:
        edges = jnp.concatenate([lists, rep_swap(lists)], axis=0)
    else:
        edges = lax.all_gather(lists, "rep", axis=0, tiled=True)
    meta = edges[:, 3 * slots, :TILE]

    def list_place(offset, which):
        group = offset // per
        group = group ^ replica if groups == 2 else group
        return (2 * group + which) * per + offset % per

    position = jnp.where(chip % 2 == 0, chip // 2, lanes - 1 - chip // 2)

    def pairs_of(distances):
        places = []
        for distance in distances:
            there = (position + distance + lanes) % lanes
            source = jnp.where(there < layers, 2 * there, 2 * (lanes - 1 - there) + 1)
            places.append(list_place((chip - source + lanes) % lanes, 0))
            places.append(list_place((chip - source - core + lanes) % lanes, 1))
        return jnp.stack(places).astype(jnp.int32)

    tiles_per = rows // TILE
    tiles_here = shard // TILE
    rotation = (tiles_per - replica * tiles_here) if groups == 2 else 0 * replica
    place = jnp.stack([replica * tiles_here, rotation]).astype(jnp.int32)
    add = functools.partial(add_sources, rows=rows, slots=slots)

    root = jnp.dot(features, root_weight, precision=highest) + bias

    half = shard // 2
    up, down = own, own
    totals = add(pairs_of([0]), place, meta, edges, [[[v] for v in own]], None)
    for step in range(1, lanes // 2 - 1):
        up, down = [ring(v, 1) for v in up], [ring(v, -1) for v in down]
        parts = [[[v] for v in up], [[v] for v in down]]
        totals = add(pairs_of([-step, step]), place, meta, edges, parts, totals)
    step = lanes // 2 - 1
    pairs = pairs_of([-step, step])
    up, down = [ring(v, 1) for v in up], [ring(v, -1) for v in down]
    totals = list(totals)
    ends = []
    for f in range(chunks):
        up[f], down[f], totals = lax.optimization_barrier((up[f], down[f], list(totals)))
        totals = list(totals)
        ends.append([ring(up[f][:half], 1), ring(down[f][half:], -1)])
        totals[f : f + 1] = add(pairs, place, meta, edges, [[[up[f]]], [[down[f]]]], totals[f : f + 1])
    pairs = pairs_of([lanes // 2])
    hidden = root
    for f in range(chunks):
        own_sum, sibling_sum = add(pairs, place, meta, edges, [[ends[f]]], [totals[f]], last=True)
        swapped = core_swap(sibling_sum)
        if groups == 2:
            other = rep_swap(own_sum[shard:] + swapped[shard:])
            share = own_sum[:shard] + swapped[:shard] + other
        else:
            share = lax.psum_scatter(own_sum + swapped, "rep", scatter_dimension=0, tiled=True)
        mixed = share * scale[:, None]
        hidden = hidden + jnp.dot(mixed, neighbor_weight[f * TILE : (f + 1) * TILE], precision=highest)
    return jax.nn.relu(hidden)


def solution(mesh):
    placed = (
        P(("blk", "rep"), None),
        P(("blk", "rep")),
        P(),
        P(),
        P(),
        P("blk", "rep", None),
        P("blk", "rep", None),
        P("blk", "rep"),
        P("blk", "rep", None, None),
        P("blk", "rep", None, None),
        P("blk", "rep", None, None),
    )
    return jax.shard_map(
        on_device, mesh=mesh, in_specs=placed, out_specs=P(("blk", "rep"), None), check_vma=False
    )
```

```python
import functools

import jax
import jax.numpy as jnp
from jax import lax
from jax.experimental import pallas as pl
from jax.experimental.pallas import tpu as pltpu
from jax.sharding import PartitionSpec as P

TILE = 128
UNROLL = 8
SMEM = pl.BlockSpec(memory_space=pltpu.SMEM)
VMEM = pl.BlockSpec(memory_space=pltpu.VMEM)


def bf16_pair(value):
    high = value.astype(jnp.bfloat16)
    low = (value - high.astype(jnp.float32)).astype(jnp.bfloat16)
    return high, low


def tile_matrix(edges, pair, slot, slots, live):
    rows = edges[pair, pl.ds(slot, 1), :]
    cols = edges[pair, pl.ds(slot + slots, 1), :]
    weights = edges[pair, pl.ds(slot + 2 * slots, 1), :]
    weights = jnp.where(live, weights, 0).astype(jnp.float32)
    index = lax.broadcasted_iota(jnp.int32, (TILE, rows.shape[1]), 0)
    row_hot = jnp.where(index == rows, 1.0, 0.0).astype(jnp.bfloat16)
    col_hot = jnp.where(index == cols, weights, 0.0).astype(jnp.bfloat16)
    matrix = lax.dot_general(
        row_hot, col_hot, (((1,), (1,)), ((), ())), preferred_element_type=jnp.float32
    )
    return jnp.concatenate(bf16_pair(matrix), axis=1)


def sum_kernel(sources, chunks, pieces, slots, first, last, *refs):
    pairs, place, meta, edges = refs[:4]
    refs = refs[4:]
    count = sources * chunks * pieces
    parts, refs = refs[:count], refs[count:]
    if not first:
        before, refs = refs[:chunks], refs[chunks:]
    if last:
        outs, sides, entries = refs[: 2 * chunks], refs[2 * chunks], refs[2 * chunks + 1]
        sums = refs[2 * chunks + 2 :]
    else:
        sums, sides, entries = refs[:chunks], refs[chunks], refs[chunks + 1]
    tiles_here = sides.shape[1]
    tiles_per = sums[0].shape[1] // TILE

    for chunk in range(chunks):
        if first:
            sums[chunk][...] = jnp.zeros_like(sums[chunk])
        elif last:
            sums[chunk][...] = before[chunk][...]

    used = jnp.int32(0)
    for number in range(2 * sources):
        pair = pairs[number]
        for slot in range(slots):
            column = meta[pair, slots + slot] - place[0]
            row = (meta[pair, slot] + place[1]) & (tiles_per - 1)
            wanted = (slot < meta[pair, 2 * slots]) & (column >= 0) & (column < tiles_here)
            code = ((number * slots + slot) * tiles_here + column) * tiles_per + row
            entries[used] = jnp.where(wanted, code, 0)
            used = used + wanted.astype(jnp.int32)
    for extra in range(UNROLL - 1):
        entries[used + extra] = 0

    for source in range(sources):
        for chunk in range(chunks):
            left = 2 * TILE * chunk
            for piece in range(pieces):
                part = parts[(source * chunks + chunk) * pieces + piece]
                size = min(part.shape[0], TILE)
                for start in range(0, part.shape[0], size):
                    at = piece * part.shape[0] + start
                    high, low = bf16_pair(part[start : start + size, :])
                    for half in range(2):
                        below = half * TILE + at % TILE
                        sides[source, at // TILE, below : below + size, left : left + TILE] = high
                        sides[source, at // TILE, below : below + size, left + TILE : left + 2 * TILE] = low

    def group(step, carry):
        todo = []
        for lane in range(UNROLL):
            entry = step * UNROLL + lane
            code = entries[entry]
            row = code & (tiles_per - 1)
            code = lax.div(code, tiles_per)
            column = lax.rem(code, tiles_here)
            code = lax.div(code, tiles_here)
            slot = lax.rem(code, slots)
            number = lax.div(code, slots)
            matrix = tile_matrix(edges, pairs[number], slot, slots, entry < used)
            todo.append((matrix, number, column, row))
        results = [
            jnp.dot(matrix, sides[lax.div(number, 2), column], preferred_element_type=jnp.float32)
            for matrix, number, column, _ in todo
        ]
        for (_, number, _, row), result in zip(todo, results):
            at = (lax.rem(number, 2), pl.ds(pl.multiple_of(row * TILE, TILE), TILE), slice(None))
            for chunk in range(chunks):
                left = 2 * TILE * chunk
                sums[chunk][at] += result[:, left : left + TILE] + result[:, left + TILE : left + 2 * TILE]
        return carry

    lax.fori_loop(0, lax.div(used + UNROLL - 1, UNROLL), group, 0)
    if last:
        for chunk in range(chunks):
            for block in range(2):
                outs[2 * chunk + block][...] = sums[chunk][block]


def add_sources(pairs, place, meta, edges, parts, before, rows, slots, last=False):
    sources, chunks, pieces = len(parts), len(parts[0]), len(parts[0][0])
    flat = [piece for source in parts for chunk in source for piece in chunk]
    here, width = pieces * flat[0].shape[0], flat[0].shape[1]
    first = before is None
    whole = jax.ShapeDtypeStruct((2, rows, width), jnp.float32)
    block = jax.ShapeDtypeStruct((rows, width), jnp.float32)
    olds = [] if first else list(before)
    outs = [block] * (2 * chunks) if last else [pltpu.VMEM(whole.shape, whole.dtype)] * chunks
    scratch = [
        pltpu.VMEM((sources, here // TILE, 2 * TILE, 2 * TILE * chunks), jnp.bfloat16),
        pltpu.SMEM((2 * sources * slots + UNROLL,), jnp.int32),
    ]
    aliases = {}
    if last:
        scratch += [pltpu.VMEM(whole.shape, jnp.float32)] * chunks
    elif not first:
        olds = [pltpu.with_memory_space_constraint(old, pltpu.VMEM) for old in olds]
        aliases = {4 + len(flat) + chunk: chunk for chunk in range(chunks)}
    flops = 1_000_000_000 * (1 + sources * chunks)
    return pl.pallas_call(
        functools.partial(sum_kernel, sources, chunks, pieces, slots, first, last),
        in_specs=[SMEM] * 3 + [VMEM] * (1 + len(flat) + len(olds)),
        out_specs=[VMEM] * len(outs),
        out_shape=outs,
        scratch_shapes=scratch,
        input_output_aliases=aliases,
        compiler_params=pltpu.CompilerParams(vmem_limit_bytes=24 << 20),
        cost_estimate=pl.CostEstimate(flops=flops, bytes_accessed=1 << 20, transcendentals=0),
    )(pairs, place, meta, edges, *flat, *olds)


def on_device(
    features,
    degrees,
    root_weight,
    neighbor_weight,
    bias,
    tile_rows,
    tile_cols,
    tile_count,
    edge_row,
    edge_col,
    edge_weight,
):
    highest = lax.Precision.HIGHEST
    groups, blocks = lax.axis_size("rep"), lax.axis_size("blk")
    lanes = blocks // 2
    layers = lanes // 2
    arc, slots, listed = edge_row.shape[1:]
    per = arc // 2
    shard, width = features.shape
    rows = shard * groups
    chunks = width // TILE
    block, replica = lax.axis_index("blk"), lax.axis_index("rep")
    chip, core = block // 2, block % 2

    def chip_at(position):
        return 2 * position if position < layers else 2 * (lanes - 1 - position) + 1

    def ring(value, step):
        pairs = [
            (2 * chip_at(p) + c, 2 * chip_at((p + step) % lanes) + c) for p in range(lanes) for c in range(2)
        ]
        return lax.ppermute(value, "blk", pairs)

    def core_swap(value):
        return lax.ppermute(value, "blk", [(b, b ^ 1) for b in range(blocks)])

    def rep_swap(value):
        return lax.ppermute(value, "rep", [(0, 1), (1, 0)])

    scale = lax.rsqrt(degrees.astype(jnp.float32))
    scaled = features * scale[:, None]
    own = [scaled[:, f * TILE : (f + 1) * TILE] for f in range(chunks)]

    def bundle(start):
        lists = [array[0, start::2] for array in (edge_row, edge_col, edge_weight)]
        head = jnp.concatenate(
            [tile_rows[0, start::2], tile_cols[0, start::2], tile_count[0, start::2, None]], axis=1
        )
        head = jnp.pad(head, ((0, 0), (0, listed - head.shape[1])))[:, None]
        head = jnp.pad(head, ((0, 0), (0, 7), (0, 0)))
        return jnp.concatenate(lists + [head], axis=1)

    lists = jnp.concatenate([bundle(0), core_swap(bundle(1))], axis=0)
    if groups == 2:
        edges = jnp.concatenate([lists, rep_swap(lists)], axis=0)
    else:
        edges = lax.all_gather(lists, "rep", axis=0, tiled=True)
    meta = edges[:, 3 * slots, :TILE]

    def list_place(offset, which):
        group = offset // per
        group = group ^ replica if groups == 2 else group
        return (2 * group + which) * per + offset % per

    position = jnp.where(chip % 2 == 0, chip // 2, lanes - 1 - chip // 2)

    def pairs_of(distances):
        places = []
        for distance in distances:
            there = (position + distance + lanes) % lanes
            source = jnp.where(there < layers, 2 * there, 2 * (lanes - 1 - there) + 1)
            places.append(list_place((chip - source + lanes) % lanes, 0))
            places.append(list_place((chip - source - core + lanes) % lanes, 1))
        return jnp.stack(places).astype(jnp.int32)

    tiles_per = rows // TILE
    tiles_here = shard // TILE
    rotation = (tiles_per - replica * tiles_here) if groups == 2 else 0 * replica
    place = jnp.stack([replica * tiles_here, rotation]).astype(jnp.int32)
    add = functools.partial(add_sources, rows=rows, slots=slots)

    root = jnp.dot(features, root_weight, precision=highest) + bias

    half = shard // 2
    half = shard // 2
    hops = [(own, own)]
    totals = None
    for step in range(1, lanes // 2):
        up, down = hops[-1]
        if totals is not None:
            up, down = list(up), list(down)
            up[-1], down[-1], totals = lax.optimization_barrier((up[-1], down[-1], totals))
        hops.append(([ring(v, 1) for v in up], [ring(v, -1) for v in down]))
        if step == 2:
            totals = add(pairs_of([0]), place, meta, edges, [[[v] for v in own]], None)
        if step >= 2:
            parts = [[[v] for v in side] for side in hops[step - 1]]
            totals = add(pairs_of([1 - step, step - 1]), place, meta, edges, parts, totals)
    up, down = [list(side) for side in hops[-1]]
    up[-1], down[-1], totals = lax.optimization_barrier((up[-1], down[-1], totals))
    ends = [[ring(up[f][:half], 1), ring(down[f][half:], -1)] for f in range(chunks)]
    step = lanes // 2 - 1
    totals = add(pairs_of([-step, step]), place, meta, edges, [[[v] for v in up], [[v] for v in down]], totals)
    pairs = pairs_of([lanes // 2])
    hidden = root
    for f in range(chunks):
        own_sum, sibling_sum = add(pairs, place, meta, edges, [[ends[f]]], [totals[f]], last=True)
        if f + 1 < chunks:
            totals, sibling_sum = lax.optimization_barrier((list(totals), sibling_sum))
        swapped = core_swap(sibling_sum)
        if groups == 2:
            other = rep_swap(own_sum[shard:] + swapped[shard:])
            share = own_sum[:shard] + swapped[:shard] + other
        else:
            share = lax.psum_scatter(own_sum + swapped, "rep", scatter_dimension=0, tiled=True)
        mixed = share * scale[:, None]
        hidden = hidden + jnp.dot(mixed, neighbor_weight[f * TILE : (f + 1) * TILE], precision=highest)
    return jax.nn.relu(hidden)


def solution(mesh):
    placed = (
        P(("blk", "rep"), None),
        P(("blk", "rep")),
        P(),
        P(),
        P(),
        P("blk", "rep", None),
        P("blk", "rep", None),
        P("blk", "rep"),
        P("blk", "rep", None, None),
        P("blk", "rep", None, None),
        P("blk", "rep", None, None),
    )
    return jax.shard_map(
        on_device, mesh=mesh, in_specs=placed, out_specs=P(("blk", "rep"), None), check_vma=False
    )
```

```python
import functools

import jax
import jax.numpy as jnp
from jax import lax
from jax.experimental import pallas as pl
from jax.experimental.pallas import tpu as pltpu
from jax.sharding import PartitionSpec as P

TILE = 128
UNROLL = 8
SMEM = pl.BlockSpec(memory_space=pltpu.SMEM)
VMEM = pl.BlockSpec(memory_space=pltpu.VMEM)


def bf16_pair(value):
    high = value.astype(jnp.bfloat16)
    low = (value - high.astype(jnp.float32)).astype(jnp.bfloat16)
    return high, low


def tile_matrix(edges, pair, slot, slots, live):
    rows = edges[pair, pl.ds(slot, 1), :]
    cols = edges[pair, pl.ds(slot + slots, 1), :]
    weights = edges[pair, pl.ds(slot + 2 * slots, 1), :]
    weights = jnp.where(live, weights, 0).astype(jnp.float32)
    index = lax.broadcasted_iota(jnp.int32, (TILE, rows.shape[1]), 0)
    row_hot = jnp.where(index == rows, 1.0, 0.0).astype(jnp.bfloat16)
    col_hot = jnp.where(index == cols, weights, 0.0).astype(jnp.bfloat16)
    matrix = lax.dot_general(
        row_hot, col_hot, (((1,), (1,)), ((), ())), preferred_element_type=jnp.float32
    )
    return jnp.concatenate(bf16_pair(matrix), axis=1)


def sum_kernel(sources, chunks, pieces, slots, first, last, *refs):
    pairs, place, meta, edges = refs[:4]
    refs = refs[4:]
    count = sources * chunks * pieces
    parts, refs = refs[:count], refs[count:]
    if not first:
        before, refs = refs[:chunks], refs[chunks:]
    if last:
        outs, sides, entries = refs[: 2 * chunks], refs[2 * chunks], refs[2 * chunks + 1]
        sums = refs[2 * chunks + 2 :]
    else:
        sums, sides, entries = refs[:chunks], refs[chunks], refs[chunks + 1]
    tiles_here = sides.shape[1]
    tiles_per = sums[0].shape[1] // TILE

    for chunk in range(chunks):
        if first:
            sums[chunk][...] = jnp.zeros_like(sums[chunk])
        elif last:
            sums[chunk][...] = before[chunk][...]

    used = jnp.int32(0)
    for number in range(2 * sources):
        pair = pairs[number]
        for slot in range(slots):
            column = meta[pair, slots + slot] - place[0]
            row = (meta[pair, slot] + place[1]) & (tiles_per - 1)
            wanted = (slot < meta[pair, 2 * slots]) & (column >= 0) & (column < tiles_here)
            code = ((number * slots + slot) * tiles_here + column) * tiles_per + row
            entries[used] = jnp.where(wanted, code, 0)
            used = used + wanted.astype(jnp.int32)
    for extra in range(UNROLL - 1):
        entries[used + extra] = 0

    for source in range(sources):
        for chunk in range(chunks):
            left = 2 * TILE * chunk
            for piece in range(pieces):
                part = parts[(source * chunks + chunk) * pieces + piece]
                size = min(part.shape[0], TILE)
                for start in range(0, part.shape[0], size):
                    at = piece * part.shape[0] + start
                    high, low = bf16_pair(part[start : start + size, :])
                    for half in range(2):
                        below = half * TILE + at % TILE
                        sides[source, at // TILE, below : below + size, left : left + TILE] = high
                        sides[source, at // TILE, below : below + size, left + TILE : left + 2 * TILE] = low

    def group(step, carry):
        todo = []
        for lane in range(UNROLL):
            entry = step * UNROLL + lane
            code = entries[entry]
            row = code & (tiles_per - 1)
            code = lax.div(code, tiles_per)
            column = lax.rem(code, tiles_here)
            code = lax.div(code, tiles_here)
            slot = lax.rem(code, slots)
            number = lax.div(code, slots)
            matrix = tile_matrix(edges, pairs[number], slot, slots, entry < used)
            todo.append((matrix, number, column, row))
        results = [
            jnp.dot(matrix, sides[lax.div(number, 2), column], preferred_element_type=jnp.float32)
            for matrix, number, column, _ in todo
        ]
        for (_, number, _, row), result in zip(todo, results):
            at = (lax.rem(number, 2), pl.ds(pl.multiple_of(row * TILE, TILE), TILE), slice(None))
            for chunk in range(chunks):
                left = 2 * TILE * chunk
                sums[chunk][at] += result[:, left : left + TILE] + result[:, left + TILE : left + 2 * TILE]
        return carry

    lax.fori_loop(0, lax.div(used + UNROLL - 1, UNROLL), group, 0)
    if last:
        for chunk in range(chunks):
            for block in range(2):
                outs[2 * chunk + block][...] = sums[chunk][block]


def add_sources(pairs, place, meta, edges, parts, before, rows, slots, last=False):
    sources, chunks, pieces = len(parts), len(parts[0]), len(parts[0][0])
    flat = [piece for source in parts for chunk in source for piece in chunk]
    here, width = pieces * flat[0].shape[0], flat[0].shape[1]
    first = before is None
    whole = jax.ShapeDtypeStruct((2, rows, width), jnp.float32)
    block = jax.ShapeDtypeStruct((rows, width), jnp.float32)
    olds = [] if first else list(before)
    outs = [block] * (2 * chunks) if last else [pltpu.VMEM(whole.shape, whole.dtype)] * chunks
    scratch = [
        pltpu.VMEM((sources, here // TILE, 2 * TILE, 2 * TILE * chunks), jnp.bfloat16),
        pltpu.SMEM((2 * sources * slots + UNROLL,), jnp.int32),
    ]
    aliases = {}
    if last:
        scratch += [pltpu.VMEM(whole.shape, jnp.float32)] * chunks
    elif not first:
        olds = [pltpu.with_memory_space_constraint(old, pltpu.VMEM) for old in olds]
        aliases = {4 + len(flat) + chunk: chunk for chunk in range(chunks)}
    flops = 1_000_000_000 * (1 + sources * chunks)
    return pl.pallas_call(
        functools.partial(sum_kernel, sources, chunks, pieces, slots, first, last),
        in_specs=[SMEM] * 3 + [VMEM] * (1 + len(flat) + len(olds)),
        out_specs=[VMEM] * len(outs),
        out_shape=outs,
        scratch_shapes=scratch,
        input_output_aliases=aliases,
        compiler_params=pltpu.CompilerParams(vmem_limit_bytes=24 << 20),
        cost_estimate=pl.CostEstimate(flops=flops, bytes_accessed=1 << 20, transcendentals=0),
    )(pairs, place, meta, edges, *flat, *olds)


def on_device(
    features,
    degrees,
    root_weight,
    neighbor_weight,
    bias,
    tile_rows,
    tile_cols,
    tile_count,
    edge_row,
    edge_col,
    edge_weight,
):
    highest = lax.Precision.HIGHEST
    groups, blocks = lax.axis_size("rep"), lax.axis_size("blk")
    lanes = blocks // 2
    layers = lanes // 2
    arc, slots, listed = edge_row.shape[1:]
    per = arc // 2
    shard, width = features.shape
    rows = shard * groups
    chunks = width // TILE
    block, replica = lax.axis_index("blk"), lax.axis_index("rep")
    chip, core = block // 2, block % 2

    def chip_at(position):
        return 2 * position if position < layers else 2 * (lanes - 1 - position) + 1

    def ring(value, step):
        pairs = [
            (2 * chip_at(p) + c, 2 * chip_at((p + step) % lanes) + c) for p in range(lanes) for c in range(2)
        ]
        return lax.ppermute(value, "blk", pairs)

    def core_swap(value):
        return lax.ppermute(value, "blk", [(b, b ^ 1) for b in range(blocks)])

    def rep_swap(value):
        return lax.ppermute(value, "rep", [(0, 1), (1, 0)])

    scale = lax.rsqrt(degrees.astype(jnp.float32))
    scaled = features * scale[:, None]
    own = [scaled[:, f * TILE : (f + 1) * TILE] for f in range(chunks)]

    def bundle(start):
        lists = [array[0, start::2] for array in (edge_row, edge_col, edge_weight)]
        head = jnp.concatenate(
            [tile_rows[0, start::2], tile_cols[0, start::2], tile_count[0, start::2, None]], axis=1
        )
        head = jnp.pad(head, ((0, 0), (0, listed - head.shape[1])))[:, None]
        head = jnp.pad(head, ((0, 0), (0, 7), (0, 0)))
        return jnp.concatenate(lists + [head], axis=1)

    lists = jnp.concatenate([bundle(0), core_swap(bundle(1))], axis=0)
    if groups == 2:
        edges = jnp.concatenate([lists, rep_swap(lists)], axis=0)
    else:
        edges = lax.all_gather(lists, "rep", axis=0, tiled=True)
    meta = edges[:, 3 * slots, :TILE]

    def list_place(offset, which):
        group = offset // per
        group = group ^ replica if groups == 2 else group
        return (2 * group + which) * per + offset % per

    position = jnp.where(chip % 2 == 0, chip // 2, lanes - 1 - chip // 2)

    def pairs_of(distances):
        places = []
        for distance in distances:
            there = (position + distance + lanes) % lanes
            source = jnp.where(there < layers, 2 * there, 2 * (lanes - 1 - there) + 1)
            places.append(list_place((chip - source + lanes) % lanes, 0))
            places.append(list_place((chip - source - core + lanes) % lanes, 1))
        return jnp.stack(places).astype(jnp.int32)

    tiles_per = rows // TILE
    tiles_here = shard // TILE
    rotation = (tiles_per - replica * tiles_here) if groups == 2 else 0 * replica
    place = jnp.stack([replica * tiles_here, rotation]).astype(jnp.int32)
    add = functools.partial(add_sources, rows=rows, slots=slots)

    root = jnp.dot(features, root_weight, precision=highest) + bias

    half = shard // 2
    half = shard // 2
    hops = [(own, own)]
    totals = None
    for step in range(1, lanes // 2):
        up, down = hops[-1]
        if totals is not None:
            up, down = list(up), list(down)
            up[0], down[0], totals = lax.optimization_barrier((up[0], down[0], totals))
        hops.append(([ring(v, 1) for v in up], [ring(v, -1) for v in down]))
        if step == 2:
            totals = add(pairs_of([0]), place, meta, edges, [[[v] for v in own]], None)
        if step >= 2:
            parts = [[[v] for v in side] for side in hops[step - 1]]
            totals = add(pairs_of([1 - step, step - 1]), place, meta, edges, parts, totals)
    up, down = [list(side) for side in hops[-1]]
    up[0], down[0], totals = lax.optimization_barrier((up[0], down[0], totals))
    ends = [[ring(up[f][:half], 1), ring(down[f][half:], -1)] for f in range(chunks)]
    step = lanes // 2 - 1
    totals = add(pairs_of([-step, step]), place, meta, edges, [[[v] for v in up], [[v] for v in down]], totals)
    pairs = pairs_of([lanes // 2])
    hidden = root
    for f in range(chunks):
        own_sum, sibling_sum = add(pairs, place, meta, edges, [[ends[f]]], [totals[f]], last=True)
        swapped = core_swap(sibling_sum)
        if groups == 2:
            other = rep_swap(own_sum[shard:] + swapped[shard:])
            share = own_sum[:shard] + swapped[:shard] + other
        else:
            share = lax.psum_scatter(own_sum + swapped, "rep", scatter_dimension=0, tiled=True)
        mixed = share * scale[:, None]
        hidden = hidden + jnp.dot(mixed, neighbor_weight[f * TILE : (f + 1) * TILE], precision=highest)
    return jax.nn.relu(hidden)


def solution(mesh):
    placed = (
        P(("blk", "rep"), None),
        P(("blk", "rep")),
        P(),
        P(),
        P(),
        P("blk", "rep", None),
        P("blk", "rep", None),
        P("blk", "rep"),
        P("blk", "rep", None, None),
        P("blk", "rep", None, None),
        P("blk", "rep", None, None),
    )
    return jax.shard_map(
        on_device, mesh=mesh, in_specs=placed, out_specs=P(("blk", "rep"), None), check_vma=False
    )
```

```python
import functools

import jax
import jax.numpy as jnp
import numpy as np
from jax import lax
from jax.experimental import pallas as pl
from jax.experimental.pallas import tpu as pltpu
from jax.sharding import PartitionSpec as P

TILE = 128
UNROLL = 8
SMEM = pl.BlockSpec(memory_space=pltpu.SMEM)
VMEM = pl.BlockSpec(memory_space=pltpu.VMEM)


def bf16_pair(value):
    high = value.astype(jnp.bfloat16)
    low = (value - high.astype(jnp.float32)).astype(jnp.bfloat16)
    return high, low


def scale_kernel(degrees, features, *outs):
    factor = lax.rsqrt(degrees[...].astype(jnp.float32))
    for tile in range(degrees.shape[0]):
        rows = slice(tile * TILE, (tile + 1) * TILE)
        column = jnp.transpose(jnp.broadcast_to(factor[tile : tile + 1, :], (TILE, TILE)))
        outs[0][rows, :] = features[rows, :] * column
        if len(outs) > 1:
            outs[1][rows, :] = column


def scaled_chunk(degrees, features, chunk, wide=False):
    rows = features.shape[0]
    tiles = rows // TILE
    outs = 2 if wide else 1
    return pl.pallas_call(
        scale_kernel,
        grid=(1,),
        in_specs=[
            pl.BlockSpec((tiles, TILE), lambda step: (0, 0)),
            pl.BlockSpec((rows, TILE), lambda step: (0, chunk)),
        ],
        out_specs=[pl.BlockSpec((rows, TILE), lambda step: (0, 0))] * outs,
        out_shape=[pltpu.VMEM((rows, TILE), jnp.float32)] * outs,
        cost_estimate=pl.CostEstimate(flops=3_000_000_000, bytes_accessed=1 << 20, transcendentals=0),
    )(degrees.reshape(tiles, TILE), features)


def tile_matrix(edges, pair, slot, slots, live):
    rows = edges[pair, pl.ds(slot, 1), :]
    cols = edges[pair, pl.ds(slot + slots, 1), :]
    weights = edges[pair, pl.ds(slot + 2 * slots, 1), :]
    weights = jnp.where(live, weights, 0).astype(jnp.float32)
    index = lax.broadcasted_iota(jnp.int32, (TILE, rows.shape[1]), 0)
    row_hot = jnp.where(index == rows, 1.0, 0.0).astype(jnp.bfloat16)
    col_hot = jnp.where(index == cols, weights, 0.0).astype(jnp.bfloat16)
    matrix = lax.dot_general(
        row_hot, col_hot, (((1,), (1,)), ((), ())), preferred_element_type=jnp.float32
    )
    return jnp.concatenate(bf16_pair(matrix), axis=1)


def sum_kernel(base, sources, chunks, pieces, slots, first, last, *refs):
    numbers, meta, edges = refs[:3]
    refs = refs[3:]
    count = sources * chunks * pieces
    parts, refs = refs[:count], refs[count:]
    if not first:
        before, refs = refs[:chunks], refs[chunks:]
    if last:
        outs, sides, entries = refs[: 2 * chunks], refs[2 * chunks], refs[2 * chunks + 1]
        sums = refs[2 * chunks + 2 :]
    else:
        sums, sides, entries = refs[:chunks], refs[chunks], refs[chunks + 1]
    tiles_here = sides.shape[1]
    tiles_per = sums[0].shape[1] // TILE

    for chunk in range(chunks):
        if first:
            sums[chunk][...] = jnp.zeros_like(sums[chunk])
        elif last:
            sums[chunk][...] = before[chunk][...]

    used = jnp.int32(0)
    for number in range(2 * sources):
        pair = jnp.maximum(numbers[base + number], 0)
        listed = numbers[base + number] >= 0
        for slot in range(slots):
            column = meta[pair, slots + slot] - numbers[0]
            row = (meta[pair, slot] + numbers[1]) & (tiles_per - 1)
            wanted = listed & (slot < meta[pair, 2 * slots]) & (column >= 0) & (column < tiles_here)
            code = ((number * slots + slot) * tiles_here + column) * tiles_per + row
            entries[used] = jnp.where(wanted, code, 0)
            used = used + wanted.astype(jnp.int32)
    for extra in range(UNROLL - 1):
        entries[used + extra] = 0

    for source in range(sources):
        for chunk in range(chunks):
            left = 2 * TILE * chunk
            for piece in range(pieces):
                part = parts[(source * chunks + chunk) * pieces + piece]
                size = min(part.shape[0], TILE)
                for start in range(0, part.shape[0], size):
                    at = piece * part.shape[0] + start
                    high, low = bf16_pair(part[start : start + size, :])
                    for half in range(2):
                        below = half * TILE + at % TILE
                        sides[source, at // TILE, below : below + size, left : left + TILE] = high
                        sides[source, at // TILE, below : below + size, left + TILE : left + 2 * TILE] = low

    def group(step, carry):
        todo = []
        for lane in range(UNROLL):
            entry = step * UNROLL + lane
            code = entries[entry]
            row = code & (tiles_per - 1)
            code = lax.div(code, tiles_per)
            column = lax.rem(code, tiles_here)
            code = lax.div(code, tiles_here)
            slot = lax.rem(code, slots)
            number = lax.div(code, slots)
            pair = jnp.maximum(numbers[base + number], 0)
            matrix = tile_matrix(edges, pair, slot, slots, entry < used)
            todo.append((matrix, number, column, row))
        results = [
            jnp.dot(matrix, sides[lax.div(number, 2), column], preferred_element_type=jnp.float32)
            for matrix, number, column, _ in todo
        ]
        for (_, number, _, row), result in zip(todo, results):
            at = (lax.rem(number, 2), pl.ds(pl.multiple_of(row * TILE, TILE), TILE), slice(None))
            for chunk in range(chunks):
                left = 2 * TILE * chunk
                sums[chunk][at] += result[:, left : left + TILE] + result[:, left + TILE : left + 2 * TILE]
        return carry

    lax.fori_loop(0, lax.div(used + UNROLL - 1, UNROLL), group, 0)
    if last:
        for chunk in range(chunks):
            for block in range(2):
                outs[2 * chunk + block][...] = sums[chunk][block]


def add_sources(base, numbers, meta, edges, parts, before, rows, slots, last=False):
    sources, chunks, pieces = len(parts), len(parts[0]), len(parts[0][0])
    flat = [piece for source in parts for chunk in source for piece in chunk]
    here, width = pieces * flat[0].shape[0], flat[0].shape[1]
    first = before is None
    whole = jax.ShapeDtypeStruct((2, rows, width), jnp.float32)
    block = jax.ShapeDtypeStruct((rows, width), jnp.float32)
    olds = [] if first else list(before)
    outs = [block] * (2 * chunks) if last else [pltpu.VMEM(whole.shape, whole.dtype)] * chunks
    scratch = [
        pltpu.VMEM((sources, here // TILE, 2 * TILE, 2 * TILE * chunks), jnp.bfloat16),
        pltpu.SMEM((2 * sources * slots + UNROLL,), jnp.int32),
    ]
    aliases = {}
    if last:
        scratch += [pltpu.VMEM(whole.shape, jnp.float32)] * chunks
    elif not first:
        olds = [pltpu.with_memory_space_constraint(old, pltpu.VMEM) for old in olds]
        aliases = {3 + len(flat) + chunk: chunk for chunk in range(chunks)}
    flops = 1_000_000_000 * (2 if last else 1) * (1 + sources * chunks)
    return pl.pallas_call(
        functools.partial(sum_kernel, base, sources, chunks, pieces, slots, first, last),
        in_specs=[SMEM] * 2 + [VMEM] * (1 + len(flat) + len(olds)),
        out_specs=[VMEM] * len(outs),
        out_shape=outs,
        scratch_shapes=scratch,
        input_output_aliases=aliases,
        compiler_params=pltpu.CompilerParams(vmem_limit_bytes=24 << 20),
        cost_estimate=pl.CostEstimate(flops=flops, bytes_accessed=1 << 20, transcendentals=0),
    )(numbers, meta, edges, *flat, *olds)


def on_device(
    features,
    degrees,
    root_weight,
    neighbor_weight,
    bias,
    tile_rows,
    tile_cols,
    tile_count,
    edge_row,
    edge_col,
    edge_weight,
):
    highest, final = lax.Precision.HIGHEST, lax.Precision.HIGH
    groups, blocks = lax.axis_size("rep"), lax.axis_size("blk")
    lanes = blocks // 2
    layers = lanes // 2
    arc, slots, listed = edge_row.shape[1:]
    per = arc // 2
    shard, width = features.shape
    rows = shard * groups
    chunks = width // TILE
    block, replica = lax.axis_index("blk"), lax.axis_index("rep")

    def chip_at(position):
        return 2 * position if position < layers else 2 * (lanes - 1 - position) + 1

    def ring(value, step):
        pairs = [
            (2 * chip_at(p) + c, 2 * chip_at((p + step) % lanes) + c) for p in range(lanes) for c in range(2)
        ]
        return lax.ppermute(value, "blk", pairs)

    def core_swap(value):
        return lax.ppermute(value, "blk", [(b, b ^ 1) for b in range(blocks)])

    def rep_swap(value):
        return lax.ppermute(value, "rep", [(0, 1), (1, 0)])

    (leading,) = scaled_chunk(degrees, features, chunks - 1)
    others, leading, edge_row, edge_col, edge_weight = lax.optimization_barrier(
        (features, leading, edge_row, edge_col, edge_weight)
    )
    own = [scaled_chunk(degrees, others, f, wide=f == 0) for f in range(chunks - 1)]
    wide = own[0][1]
    own = [pair[0] for pair in own] + [leading]

    def bundle(start):
        lists = [array[0, start::2] for array in (edge_row, edge_col, edge_weight)]
        head = jnp.concatenate(
            [tile_rows[0, start::2], tile_cols[0, start::2], tile_count[0, start::2, None]], axis=1
        )
        head = jnp.pad(head, ((0, 0), (0, listed - head.shape[1])))[:, None]
        head = jnp.pad(head, ((0, 0), (0, 7), (0, 0)))
        return jnp.concatenate(lists + [head], axis=1)

    lists = jnp.concatenate([bundle(0), core_swap(bundle(1))], axis=0)
    if groups == 2:
        edges = jnp.concatenate([lists, rep_swap(lists)], axis=0)
    else:
        edges = lax.all_gather(lists, "rep", axis=0, tiled=True)
    meta, near_meta = edges[:, 3 * slots, :TILE], lists[:, 3 * slots, :TILE]

    tiles_per = rows // TILE
    tiles_here = shard // TILE
    halfway = lanes // 2

    def places_of(chip, core, replica, distances, near=True, far=True):
        places = []
        for distance in distances:
            at = chip // 2 if chip % 2 == 0 else lanes - 1 - chip // 2
            source = chip_at((at + distance) % lanes)
            for which, offset in enumerate(((chip - source) % lanes, (chip - source - core) % lanes)):
                group = offset // per
                if near and not far:
                    places.append(which * per + offset % per if group == replica else -1)
                elif far and not near and group == replica:
                    places.append(-1)
                else:
                    order = group ^ replica if groups == 2 else group
                    places.append((2 * order + which) * per + offset % per)
        return places

    def numbers_of(chip, core, replica):
        rotation = tiles_per - replica * tiles_here if groups == 2 else 0
        parts = [[replica * tiles_here, rotation]]
        parts.append(places_of(chip, core, replica, [0, -1, 1], far=False))
        parts.append(places_of(chip, core, replica, [0, -1, 1], near=False))
        for step in range(2, halfway):
            parts.append(places_of(chip, core, replica, [-step, step]))
        return sum(parts + [places_of(chip, core, replica, [halfway])], [])

    table = np.array(
        [numbers_of(b // 2, b % 2, r) for b in range(blocks) for r in range(groups)], dtype=np.int32
    )
    def base_of(step):
        return 14 + 4 * (step - 2)

    add = functools.partial(add_sources, rows=rows, slots=slots)

    root = jnp.dot(features, root_weight, precision=highest) + bias

    half = shard // 2
    later = [lax.optimization_barrier((v, lists))[0] for v in own[:-1]] + own[-1:]
    hops = [(later, later)]
    for step in range(1, halfway):
        up, down = hops[-1]
        if step >= 3:
            up, down = list(up), list(down)
            up[0], down[0], totals = lax.optimization_barrier((up[0], down[0], totals))
        hops.append(([ring(v, 1) for v in up], [ring(v, -1) for v in down]))
        parts = [[[v] for v in side] for side in hops[step - 1]]
        if step == 1:
            early = parts[:1]
            index, _ = lax.optimization_barrier((block * groups + replica, hops[-1][0][0]))
            numbers = lax.dynamic_index_in_dim(jnp.asarray(table), index, keepdims=False)
        elif step == 2:
            early = early + parts
            totals = add(2, numbers, near_meta, lists, early, None)
            totals = add(8, numbers, meta, edges, early, totals)
        else:
            totals = add(base_of(step - 1), numbers, meta, edges, parts, totals)
    up, down = [list(side) for side in hops[-1]]
    up[0], down[0], totals = lax.optimization_barrier((up[0], down[0], totals))
    ends = [[ring(up[f][:half], 1), ring(down[f][half:], -1)] for f in range(chunks)]
    totals = add(base_of(halfway - 1), numbers, meta, edges, [[[v] for v in up], [[v] for v in down]], totals)
    hidden = root
    for f in range(chunks):
        own_sum, sibling_sum = add(base_of(halfway), numbers, meta, edges, [[ends[f]]], [totals[f]], last=True)
        swapped = core_swap(sibling_sum)
        if groups == 2:
            other = rep_swap(own_sum[shard:] + swapped[shard:])
            share = own_sum[:shard] + swapped[:shard] + other
        else:
            share = lax.psum_scatter(own_sum + swapped, "rep", scatter_dimension=0, tiled=True)
        mixed = share * wide
        hidden = hidden + jnp.dot(mixed, neighbor_weight[f * TILE : (f + 1) * TILE], precision=final)
    return jax.nn.relu(hidden)


def solution(mesh):
    placed = (
        P(("blk", "rep"), None),
        P(("blk", "rep")),
        P(),
        P(),
        P(),
        P("blk", "rep", None),
        P("blk", "rep", None),
        P("blk", "rep"),
        P("blk", "rep", None, None),
        P("blk", "rep", None, None),
        P("blk", "rep", None, None),
    )
    return jax.shard_map(
        on_device, mesh=mesh, in_specs=placed, out_specs=P(("blk", "rep"), None), check_vma=False
    )
```

```python
import functools

import jax
import jax.numpy as jnp
import numpy as np
from jax import lax
from jax.experimental import pallas as pl
from jax.experimental.pallas import tpu as pltpu
from jax.sharding import PartitionSpec as P

TILE = 128
UNROLL = 8
SMEM = pl.BlockSpec(memory_space=pltpu.SMEM)
VMEM = pl.BlockSpec(memory_space=pltpu.VMEM)


def bf16_pair(value):
    high = value.astype(jnp.bfloat16)
    low = (value - high.astype(jnp.float32)).astype(jnp.bfloat16)
    return high, low


def scale_kernel(degrees, features, *outs):
    factor = lax.rsqrt(degrees[...].astype(jnp.float32))
    for tile in range(degrees.shape[0]):
        rows = slice(tile * TILE, (tile + 1) * TILE)
        column = jnp.transpose(jnp.broadcast_to(factor[tile : tile + 1, :], (TILE, TILE)))
        outs[0][rows, :] = features[rows, :] * column
        if len(outs) > 1:
            outs[1][rows, :] = column


def scaled_chunk(degrees, features, chunk, wide=False):
    rows = features.shape[0]
    tiles = rows // TILE
    outs = 2 if wide else 1
    return pl.pallas_call(
        scale_kernel,
        grid=(1,),
        in_specs=[
            pl.BlockSpec((tiles, TILE), lambda step: (0, 0)),
            pl.BlockSpec((rows, TILE), lambda step: (0, chunk)),
        ],
        out_specs=[pl.BlockSpec((rows, TILE), lambda step: (0, 0))] * outs,
        out_shape=[pltpu.VMEM((rows, TILE), jnp.float32)] * outs,
        cost_estimate=pl.CostEstimate(flops=3_000_000_000, bytes_accessed=1 << 20, transcendentals=0),
    )(degrees.reshape(tiles, TILE), features)


def tile_matrix(edges, pair, slot, slots, live):
    rows = edges[pair, pl.ds(slot, 1), :]
    cols = edges[pair, pl.ds(slot + slots, 1), :]
    weights = edges[pair, pl.ds(slot + 2 * slots, 1), :]
    weights = jnp.where(live, weights, 0).astype(jnp.float32)
    index = lax.broadcasted_iota(jnp.int32, (TILE, rows.shape[1]), 0)
    row_hot = jnp.where(index == rows, 1.0, 0.0).astype(jnp.bfloat16)
    col_hot = jnp.where(index == cols, weights, 0.0).astype(jnp.bfloat16)
    matrix = lax.dot_general(
        row_hot, col_hot, (((1,), (1,)), ((), ())), preferred_element_type=jnp.float32
    )
    return jnp.concatenate(bf16_pair(matrix), axis=1)


def sum_kernel(base, sources, chunks, pieces, slots, first, last, *refs):
    numbers, meta, edges = refs[:3]
    refs = refs[3:]
    count = sources * chunks * pieces
    parts, refs = refs[:count], refs[count:]
    if not first:
        before, refs = refs[:chunks], refs[chunks:]
    if last:
        outs, sides, entries = refs[: 2 * chunks], refs[2 * chunks], refs[2 * chunks + 1]
        sums = refs[2 * chunks + 2 :]
    else:
        sums, sides, entries = refs[:chunks], refs[chunks], refs[chunks + 1]
    tiles_here = sides.shape[1]
    tiles_per = sums[0].shape[1] // TILE

    for chunk in range(chunks):
        if first:
            sums[chunk][...] = jnp.zeros_like(sums[chunk])
        elif last:
            sums[chunk][...] = before[chunk][...]

    used = jnp.int32(0)
    for number in range(2 * sources):
        pair = jnp.maximum(numbers[base + number], 0)
        listed = numbers[base + number] >= 0
        for slot in range(slots):
            column = meta[pair, slots + slot] - numbers[0]
            row = (meta[pair, slot] + numbers[1]) & (tiles_per - 1)
            wanted = listed & (slot < meta[pair, 2 * slots]) & (column >= 0) & (column < tiles_here)
            code = ((number * slots + slot) * tiles_here + column) * tiles_per + row
            entries[used] = jnp.where(wanted, code, 0)
            used = used + wanted.astype(jnp.int32)
    for extra in range(UNROLL - 1):
        entries[used + extra] = 0

    for source in range(sources):
        for chunk in range(chunks):
            left = 2 * TILE * chunk
            for piece in range(pieces):
                part = parts[(source * chunks + chunk) * pieces + piece]
                size = min(part.shape[0], TILE)
                for start in range(0, part.shape[0], size):
                    at = piece * part.shape[0] + start
                    high, low = bf16_pair(part[start : start + size, :])
                    for half in range(2):
                        below = half * TILE + at % TILE
                        sides[source, at // TILE, below : below + size, left : left + TILE] = high
                        sides[source, at // TILE, below : below + size, left + TILE : left + 2 * TILE] = low

    def group(step, carry):
        todo = []
        for lane in range(UNROLL):
            entry = step * UNROLL + lane
            code = entries[entry]
            row = code & (tiles_per - 1)
            code = lax.div(code, tiles_per)
            column = lax.rem(code, tiles_here)
            code = lax.div(code, tiles_here)
            slot = lax.rem(code, slots)
            number = lax.div(code, slots)
            pair = jnp.maximum(numbers[base + number], 0)
            matrix = tile_matrix(edges, pair, slot, slots, entry < used)
            todo.append((matrix, number, column, row))
        results = [
            jnp.dot(matrix, sides[lax.div(number, 2), column], preferred_element_type=jnp.float32)
            for matrix, number, column, _ in todo
        ]
        for (_, number, _, row), result in zip(todo, results):
            at = (lax.rem(number, 2), pl.ds(pl.multiple_of(row * TILE, TILE), TILE), slice(None))
            for chunk in range(chunks):
                left = 2 * TILE * chunk
                sums[chunk][at] += result[:, left : left + TILE] + result[:, left + TILE : left + 2 * TILE]
        return carry

    lax.fori_loop(0, lax.div(used + UNROLL - 1, UNROLL), group, 0)
    if last:
        for chunk in range(chunks):
            for block in range(2):
                outs[2 * chunk + block][...] = sums[chunk][block]


def add_sources(base, numbers, meta, edges, parts, before, rows, slots, last=False):
    sources, chunks, pieces = len(parts), len(parts[0]), len(parts[0][0])
    flat = [piece for source in parts for chunk in source for piece in chunk]
    here, width = pieces * flat[0].shape[0], flat[0].shape[1]
    first = before is None
    whole = jax.ShapeDtypeStruct((2, rows, width), jnp.float32)
    block = jax.ShapeDtypeStruct((rows, width), jnp.float32)
    olds = [] if first else list(before)
    outs = [block] * (2 * chunks) if last else [pltpu.VMEM(whole.shape, whole.dtype)] * chunks
    scratch = [
        pltpu.VMEM((sources, here // TILE, 2 * TILE, 2 * TILE * chunks), jnp.bfloat16),
        pltpu.SMEM((2 * sources * slots + UNROLL,), jnp.int32),
    ]
    aliases = {}
    if last:
        scratch += [pltpu.VMEM(whole.shape, jnp.float32)] * chunks
    elif not first:
        olds = [pltpu.with_memory_space_constraint(old, pltpu.VMEM) for old in olds]
        aliases = {3 + len(flat) + chunk: chunk for chunk in range(chunks)}
    flops = 1_000_000_000 * (2 if last else 1) * (1 + sources * chunks)
    return pl.pallas_call(
        functools.partial(sum_kernel, base, sources, chunks, pieces, slots, first, last),
        in_specs=[SMEM] * 2 + [VMEM] * (1 + len(flat) + len(olds)),
        out_specs=[VMEM] * len(outs),
        out_shape=outs,
        scratch_shapes=scratch,
        input_output_aliases=aliases,
        compiler_params=pltpu.CompilerParams(vmem_limit_bytes=24 << 20),
        cost_estimate=pl.CostEstimate(flops=flops, bytes_accessed=1 << 20, transcendentals=0),
    )(numbers, meta, edges, *flat, *olds)


def on_device(
    features,
    degrees,
    root_weight,
    neighbor_weight,
    bias,
    tile_rows,
    tile_cols,
    tile_count,
    edge_row,
    edge_col,
    edge_weight,
):
    highest, final = lax.Precision.HIGHEST, lax.Precision.HIGH
    groups, blocks = lax.axis_size("rep"), lax.axis_size("blk")
    lanes = blocks // 2
    layers = lanes // 2
    arc, slots, listed = edge_row.shape[1:]
    per = arc // 2
    shard, width = features.shape
    rows = shard * groups
    chunks = width // TILE
    block, replica = lax.axis_index("blk"), lax.axis_index("rep")

    def chip_at(position):
        return 2 * position if position < layers else 2 * (lanes - 1 - position) + 1

    def ring(value, step):
        pairs = [
            (2 * chip_at(p) + c, 2 * chip_at((p + step) % lanes) + c) for p in range(lanes) for c in range(2)
        ]
        return lax.ppermute(value, "blk", pairs)

    def core_swap(value):
        return lax.ppermute(value, "blk", [(b, b ^ 1) for b in range(blocks)])

    def rep_swap(value):
        return lax.ppermute(value, "rep", [(0, 1), (1, 0)])

    (leading,) = scaled_chunk(degrees, features, chunks - 1)
    others, leading, edge_row, edge_col, edge_weight = lax.optimization_barrier(
        (features, leading, edge_row, edge_col, edge_weight)
    )
    own = [scaled_chunk(degrees, others, f, wide=f == 0) for f in range(chunks - 1)]
    wide = own[0][1]
    own = [pair[0] for pair in own] + [leading]

    def bundle(start):
        lists = [array[0, start::2] for array in (edge_row, edge_col, edge_weight)]
        head = jnp.concatenate(
            [tile_rows[0, start::2], tile_cols[0, start::2], tile_count[0, start::2, None]], axis=1
        )
        head = jnp.pad(head, ((0, 0), (0, listed - head.shape[1])))[:, None]
        head = jnp.pad(head, ((0, 0), (0, 7), (0, 0)))
        return jnp.concatenate(lists + [head], axis=1)

    lists = jnp.concatenate([bundle(0), core_swap(bundle(1))], axis=0)
    if groups == 2:
        edges = jnp.concatenate([lists, rep_swap(lists)], axis=0)
    else:
        edges = lax.all_gather(lists, "rep", axis=0, tiled=True)
    meta, near_meta = edges[:, 3 * slots, :TILE], lists[:, 3 * slots, :TILE]

    tiles_per = rows // TILE
    tiles_here = shard // TILE
    halfway = lanes // 2

    def places_of(chip, core, replica, distances, near=True, far=True):
        places = []
        for distance in distances:
            at = chip // 2 if chip % 2 == 0 else lanes - 1 - chip // 2
            source = chip_at((at + distance) % lanes)
            for which, offset in enumerate(((chip - source) % lanes, (chip - source - core) % lanes)):
                group = offset // per
                if near and not far:
                    places.append(which * per + offset % per if group == replica else -1)
                elif far and not near and group == replica:
                    places.append(-1)
                else:
                    order = group ^ replica if groups == 2 else group
                    places.append((2 * order + which) * per + offset % per)
        return places

    def numbers_of(chip, core, replica):
        rotation = tiles_per - replica * tiles_here if groups == 2 else 0
        parts = [[replica * tiles_here, rotation]]
        parts.append(places_of(chip, core, replica, [0, -1, 1], far=False))
        parts.append(places_of(chip, core, replica, [0, -1, 1], near=False))
        for step in range(2, halfway):
            parts.append(places_of(chip, core, replica, [-step, step]))
        return sum(parts + [places_of(chip, core, replica, [halfway])], [])

    table = np.array(
        [numbers_of(b // 2, b % 2, r) for b in range(blocks) for r in range(groups)], dtype=np.int32
    )
    numbers = lax.dynamic_index_in_dim(jnp.asarray(table), block * groups + replica, keepdims=False)

    def base_of(step):
        return 14 + 4 * (step - 2)

    add = functools.partial(add_sources, rows=rows, slots=slots)

    root = jnp.dot(features, root_weight, precision=highest) + bias

    half = shard // 2
    later = [lax.optimization_barrier((v, lists))[0] for v in own[:-1]] + own[-1:]
    hops = [(later, later)]
    for step in range(1, halfway):
        up, down = hops[-1]
        if step >= 3:
            up, down = list(up), list(down)
            up[0], down[0], totals = lax.optimization_barrier((up[0], down[0], totals))
        hops.append(([ring(v, 1) for v in up], [ring(v, -1) for v in down]))
        parts = [[[v] for v in side] for side in hops[step - 1]]
        if step == 1:
            early = parts[:1]
        elif step == 2:
            early = early + parts
            totals = add(2, numbers, near_meta, lists, early, None)
            totals = add(8, numbers, meta, edges, early, totals)
        else:
            totals = add(base_of(step - 1), numbers, meta, edges, parts, totals)
    up, down = [list(side) for side in hops[-1]]
    up[0], down[0], totals = lax.optimization_barrier((up[0], down[0], totals))
    ends = [[ring(up[f][:half], 1), ring(down[f][half:], -1)] for f in range(chunks)]
    totals = add(base_of(halfway - 1), numbers, meta, edges, [[[v] for v in up], [[v] for v in down]], totals)
    hidden = root
    for f in range(chunks):
        own_sum, sibling_sum = add(base_of(halfway), numbers, meta, edges, [[ends[f]]], [totals[f]], last=True)
        swapped = core_swap(sibling_sum)
        if groups == 2:
            other = rep_swap(own_sum[shard:] + swapped[shard:])
            share = own_sum[:shard] + swapped[:shard] + other
        else:
            share = lax.psum_scatter(own_sum + swapped, "rep", scatter_dimension=0, tiled=True)
        mixed = share * wide
        hidden = hidden + jnp.dot(mixed, neighbor_weight[f * TILE : (f + 1) * TILE], precision=final)
    return jax.nn.relu(hidden)


def solution(mesh):
    placed = (
        P(("blk", "rep"), None),
        P(("blk", "rep")),
        P(),
        P(),
        P(),
        P("blk", "rep", None),
        P("blk", "rep", None),
        P("blk", "rep"),
        P("blk", "rep", None, None),
        P("blk", "rep", None, None),
        P("blk", "rep", None, None),
    )
    return jax.shard_map(
        on_device, mesh=mesh, in_specs=placed, out_specs=P(("blk", "rep"), None), check_vma=False
    )
```

```python
import functools

import jax
import jax.numpy as jnp
import numpy as np
from jax import lax
from jax.experimental import pallas as pl
from jax.experimental.pallas import tpu as pltpu
from jax.sharding import PartitionSpec as P

TILE = 128
UNROLL = 8
SMEM = pl.BlockSpec(memory_space=pltpu.SMEM)
VMEM = pl.BlockSpec(memory_space=pltpu.VMEM)


def bf16_pair(value):
    high = value.astype(jnp.bfloat16)
    low = (value - high.astype(jnp.float32)).astype(jnp.bfloat16)
    return high, low


def scale_kernel(degrees, features, *outs):
    factor = lax.rsqrt(degrees[...].astype(jnp.float32))
    for tile in range(degrees.shape[0]):
        rows = slice(tile * TILE, (tile + 1) * TILE)
        column = jnp.transpose(jnp.broadcast_to(factor[tile : tile + 1, :], (TILE, TILE)))
        outs[0][rows, :] = features[rows, :] * column
        if len(outs) > 1:
            outs[1][rows, :] = column


def scaled_chunk(degrees, features, chunk, wide=False):
    rows = features.shape[0]
    tiles = rows // TILE
    outs = 2 if wide else 1
    return pl.pallas_call(
        scale_kernel,
        grid=(1,),
        in_specs=[
            pl.BlockSpec((tiles, TILE), lambda step: (0, 0)),
            pl.BlockSpec((rows, TILE), lambda step: (0, chunk)),
        ],
        out_specs=[pl.BlockSpec((rows, TILE), lambda step: (0, 0))] * outs,
        out_shape=[pltpu.VMEM((rows, TILE), jnp.float32)] * outs,
        cost_estimate=pl.CostEstimate(flops=3_000_000_000, bytes_accessed=1 << 20, transcendentals=0),
    )(degrees.reshape(tiles, TILE), features)


def tile_matrix(edges, pair, slot, slots, live):
    rows = edges[pair, pl.ds(slot, 1), :]
    cols = edges[pair, pl.ds(slot + slots, 1), :]
    weights = edges[pair, pl.ds(slot + 2 * slots, 1), :]
    weights = jnp.where(live, weights, 0).astype(jnp.float32)
    index = lax.broadcasted_iota(jnp.int32, (TILE, rows.shape[1]), 0)
    row_hot = jnp.where(index == rows, 1.0, 0.0).astype(jnp.bfloat16)
    col_hot = jnp.where(index == cols, weights, 0.0).astype(jnp.bfloat16)
    matrix = lax.dot_general(
        row_hot, col_hot, (((1,), (1,)), ((), ())), preferred_element_type=jnp.float32
    )
    return jnp.concatenate(bf16_pair(matrix), axis=1)


def sum_kernel(base, sources, chunks, pieces, slots, first, last, *refs):
    numbers, meta, edges = refs[:3]
    refs = refs[3:]
    count = sources * chunks * pieces
    parts, refs = refs[:count], refs[count:]
    if not first:
        before, refs = refs[:chunks], refs[chunks:]
    if last:
        outs, sides, entries = refs[: 2 * chunks], refs[2 * chunks], refs[2 * chunks + 1]
        sums = refs[2 * chunks + 2 :]
    else:
        sums, sides, entries = refs[:chunks], refs[chunks], refs[chunks + 1]
    tiles_here = sides.shape[1]
    tiles_per = sums[0].shape[1] // TILE

    for chunk in range(chunks):
        if first:
            sums[chunk][...] = jnp.zeros_like(sums[chunk])
        elif last:
            sums[chunk][...] = before[chunk][...]

    used = jnp.int32(0)
    for number in range(2 * sources):
        pair = jnp.maximum(numbers[base + number], 0)
        listed = numbers[base + number] >= 0
        for slot in range(slots):
            column = meta[pair, slots + slot] - numbers[0]
            row = (meta[pair, slot] + numbers[1]) & (tiles_per - 1)
            wanted = listed & (slot < meta[pair, 2 * slots]) & (column >= 0) & (column < tiles_here)
            code = ((number * slots + slot) * tiles_here + column) * tiles_per + row
            entries[used] = jnp.where(wanted, code, 0)
            used = used + wanted.astype(jnp.int32)
    for extra in range(UNROLL - 1):
        entries[used + extra] = 0

    for source in range(sources):
        for chunk in range(chunks):
            left = 2 * TILE * chunk
            for piece in range(pieces):
                part = parts[(source * chunks + chunk) * pieces + piece]
                size = min(part.shape[0], TILE)
                for start in range(0, part.shape[0], size):
                    at = piece * part.shape[0] + start
                    high, low = bf16_pair(part[start : start + size, :])
                    for half in range(2):
                        below = half * TILE + at % TILE
                        sides[source, at // TILE, below : below + size, left : left + TILE] = high
                        sides[source, at // TILE, below : below + size, left + TILE : left + 2 * TILE] = low

    def group(step, carry):
        todo = []
        for lane in range(UNROLL):
            entry = step * UNROLL + lane
            code = entries[entry]
            row = code & (tiles_per - 1)
            code = lax.div(code, tiles_per)
            column = lax.rem(code, tiles_here)
            code = lax.div(code, tiles_here)
            slot = lax.rem(code, slots)
            number = lax.div(code, slots)
            pair = jnp.maximum(numbers[base + number], 0)
            matrix = tile_matrix(edges, pair, slot, slots, entry < used)
            todo.append((matrix, number, column, row))
        results = [
            jnp.dot(matrix, sides[lax.div(number, 2), column], preferred_element_type=jnp.float32)
            for matrix, number, column, _ in todo
        ]
        for (_, number, _, row), result in zip(todo, results):
            at = (lax.rem(number, 2), pl.ds(pl.multiple_of(row * TILE, TILE), TILE), slice(None))
            for chunk in range(chunks):
                left = 2 * TILE * chunk
                sums[chunk][at] += result[:, left : left + TILE] + result[:, left + TILE : left + 2 * TILE]
        return carry

    lax.fori_loop(0, lax.div(used + UNROLL - 1, UNROLL), group, 0)
    if last:
        for chunk in range(chunks):
            for block in range(2):
                outs[2 * chunk + block][...] = sums[chunk][block]


def add_sources(base, numbers, meta, edges, parts, before, rows, slots, last=False):
    sources, chunks, pieces = len(parts), len(parts[0]), len(parts[0][0])
    flat = [piece for source in parts for chunk in source for piece in chunk]
    here, width = pieces * flat[0].shape[0], flat[0].shape[1]
    first = before is None
    whole = jax.ShapeDtypeStruct((2, rows, width), jnp.float32)
    block = jax.ShapeDtypeStruct((rows, width), jnp.float32)
    olds = [] if first else list(before)
    outs = [block] * (2 * chunks) if last else [pltpu.VMEM(whole.shape, whole.dtype)] * chunks
    scratch = [
        pltpu.VMEM((sources, here // TILE, 2 * TILE, 2 * TILE * chunks), jnp.bfloat16),
        pltpu.SMEM((2 * sources * slots + UNROLL,), jnp.int32),
    ]
    aliases = {}
    if last:
        scratch += [pltpu.VMEM(whole.shape, jnp.float32)] * chunks
    elif not first:
        olds = [pltpu.with_memory_space_constraint(old, pltpu.VMEM) for old in olds]
        aliases = {3 + len(flat) + chunk: chunk for chunk in range(chunks)}
    flops = 1_000_000_000 * (2 if last else 1) * (1 + sources * chunks)
    return pl.pallas_call(
        functools.partial(sum_kernel, base, sources, chunks, pieces, slots, first, last),
        in_specs=[SMEM] * 2 + [VMEM] * (1 + len(flat) + len(olds)),
        out_specs=[VMEM] * len(outs),
        out_shape=outs,
        scratch_shapes=scratch,
        input_output_aliases=aliases,
        compiler_params=pltpu.CompilerParams(vmem_limit_bytes=24 << 20),
        cost_estimate=pl.CostEstimate(flops=flops, bytes_accessed=1 << 20, transcendentals=0),
    )(numbers, meta, edges, *flat, *olds)


def on_device(
    features,
    degrees,
    root_weight,
    neighbor_weight,
    bias,
    tile_rows,
    tile_cols,
    tile_count,
    edge_row,
    edge_col,
    edge_weight,
):
    highest, final = lax.Precision.HIGHEST, lax.Precision.HIGH
    groups, blocks = lax.axis_size("rep"), lax.axis_size("blk")
    lanes = blocks // 2
    layers = lanes // 2
    arc, slots, listed = edge_row.shape[1:]
    per = arc // 2
    shard, width = features.shape
    rows = shard * groups
    chunks = width // TILE
    block, replica = lax.axis_index("blk"), lax.axis_index("rep")

    def chip_at(position):
        return 2 * position if position < layers else 2 * (lanes - 1 - position) + 1

    def ring(value, step):
        pairs = [
            (2 * chip_at(p) + c, 2 * chip_at((p + step) % lanes) + c) for p in range(lanes) for c in range(2)
        ]
        return lax.ppermute(value, "blk", pairs)

    def core_swap(value):
        return lax.ppermute(value, "blk", [(b, b ^ 1) for b in range(blocks)])

    def rep_swap(value):
        return lax.ppermute(value, "rep", [(0, 1), (1, 0)])

    (leading,) = scaled_chunk(degrees, features, chunks - 1)
    others, leading, edge_row, edge_col, edge_weight = lax.optimization_barrier(
        (features, leading, edge_row, edge_col, edge_weight)
    )
    own = [scaled_chunk(degrees, others, f, wide=f == 0) for f in range(chunks - 1)]
    wide = own[0][1]
    own = [pair[0] for pair in own] + [leading]

    def bundle(start):
        lists = [array[0, start::2] for array in (edge_row, edge_col, edge_weight)]
        head = jnp.concatenate(
            [tile_rows[0, start::2], tile_cols[0, start::2], tile_count[0, start::2, None]], axis=1
        )
        head = jnp.pad(head, ((0, 0), (0, listed - head.shape[1])))[:, None]
        head = jnp.pad(head, ((0, 0), (0, 7), (0, 0)))
        return jnp.concatenate(lists + [head], axis=1)

    lists = jnp.concatenate([bundle(0), core_swap(bundle(1))], axis=0)
    if groups == 2:
        edges = jnp.concatenate([lists, rep_swap(lists)], axis=0)
    else:
        edges = lax.all_gather(lists, "rep", axis=0, tiled=True)
    meta, near_meta = edges[:, 3 * slots, :TILE], lists[:, 3 * slots, :TILE]

    tiles_per = rows // TILE
    tiles_here = shard // TILE
    halfway = lanes // 2

    def places_of(chip, core, replica, distances, near=True, far=True):
        places = []
        for distance in distances:
            at = chip // 2 if chip % 2 == 0 else lanes - 1 - chip // 2
            source = chip_at((at + distance) % lanes)
            for which, offset in enumerate(((chip - source) % lanes, (chip - source - core) % lanes)):
                group = offset // per
                if near and not far:
                    places.append(which * per + offset % per if group == replica else -1)
                elif far and not near and group == replica:
                    places.append(-1)
                else:
                    order = group ^ replica if groups == 2 else group
                    places.append((2 * order + which) * per + offset % per)
        return places

    def numbers_of(chip, core, replica):
        rotation = tiles_per - replica * tiles_here if groups == 2 else 0
        parts = [[replica * tiles_here, rotation]]
        parts.append(places_of(chip, core, replica, [0, -1, 1], far=False))
        parts.append(places_of(chip, core, replica, [0, -1, 1], near=False))
        for step in range(2, halfway):
            parts.append(places_of(chip, core, replica, [-step, step]))
        return sum(parts + [places_of(chip, core, replica, [halfway])], [])

    table = np.array(
        [numbers_of(b // 2, b % 2, r) for b in range(blocks) for r in range(groups)], dtype=np.int32
    )
    numbers = lax.dynamic_index_in_dim(jnp.asarray(table), block * groups + replica, keepdims=False)

    def base_of(step):
        return 14 + 4 * (step - 2)

    add = functools.partial(add_sources, rows=rows, slots=slots)

    root = jnp.dot(features, root_weight, precision=final) + bias

    half = shard // 2
    later = [lax.optimization_barrier((v, lists))[0] for v in own[:-1]] + own[-1:]
    hops = [(later, later)]
    for step in range(1, halfway):
        up, down = hops[-1]
        if step >= 3:
            up, down = list(up), list(down)
            up[0], down[0], totals = lax.optimization_barrier((up[0], down[0], totals))
        hops.append(([ring(v, 1) for v in up], [ring(v, -1) for v in down]))
        parts = [[[v] for v in side] for side in hops[step - 1]]
        if step == 1:
            early = parts[:1]
        elif step == 2:
            early = early + parts
            totals = add(2, numbers, near_meta, lists, early, None)
            totals = add(8, numbers, meta, edges, early, totals)
        else:
            totals = add(base_of(step - 1), numbers, meta, edges, parts, totals)
    up, down = [list(side) for side in hops[-1]]
    up[0], down[0], totals = lax.optimization_barrier((up[0], down[0], totals))
    ends = [[ring(up[f][:half], 1), ring(down[f][half:], -1)] for f in range(chunks)]
    totals = add(base_of(halfway - 1), numbers, meta, edges, [[[v] for v in up], [[v] for v in down]], totals)
    hidden = root
    for f in range(chunks):
        own_sum, sibling_sum = add(base_of(halfway), numbers, meta, edges, [[ends[f]]], [totals[f]], last=True)
        swapped = core_swap(sibling_sum)
        if groups == 2:
            other = rep_swap(own_sum[shard:] + swapped[shard:])
            share = own_sum[:shard] + swapped[:shard] + other
        else:
            share = lax.psum_scatter(own_sum + swapped, "rep", scatter_dimension=0, tiled=True)
        mixed = share * wide
        hidden = hidden + jnp.dot(mixed, neighbor_weight[f * TILE : (f + 1) * TILE], precision=final)
    return jax.nn.relu(hidden)


def solution(mesh):
    placed = (
        P(("blk", "rep"), None),
        P(("blk", "rep")),
        P(),
        P(),
        P(),
        P("blk", "rep", None),
        P("blk", "rep", None),
        P("blk", "rep"),
        P("blk", "rep", None, None),
        P("blk", "rep", None, None),
        P("blk", "rep", None, None),
    )
    return jax.shard_map(
        on_device, mesh=mesh, in_specs=placed, out_specs=P(("blk", "rep"), None), check_vma=False
    )
```
